256 devices in a mesh: dp: 4 (over y_hi, core), space: 64 (over x, z, y_lo).
Axes of the slice: x: 4, y: 4 (y_hi: 2, y_lo: 2; y = y_hi * 2 + y_lo), z: 8, core: 2. Of those that a mesh axis runs over, the one named last changes fastest.
Arguments:
- fields: bfloat16 [8, 8, 128, 128, 128], P('dp', None, 'space'), may hold values from -6 to 6
- lift_weight: bfloat16 [8, 64], replicated, may hold values from -2 to 2
- mode_weight: bfloat16 [16, 256, 64, 64], P(None, 'space'), may hold values from -0.75 to 0.75
- local_weight: bfloat16 [64, 64], replicated, may hold values from -0.75 to 0.75
- project_weight: bfloat16 [64, 8], replicated, may hold values from -0.75 to 0.75
- out_cotangent: bfloat16 [8, 8, 128, 128, 128], P('dp', None, 'space'), may hold values from -6 to 6
Outputs:
- prediction: bfloat16 [8, 8, 128, 128, 128], P('dp', None, 'space')
- mode_grad: float32 [16, 256, 64, 64], P(None, 'space')
- field_grad: bfloat16 [8, 8, 128, 128, 128], P('dp', None, 'space')
The draws below stay inside these ranges and needn't reach their ends.
All inputs are finite; a program needn't handle non-finite values.
Results may differ from the reference program's by a relative error of at most 0.025.
Values may be sent and summed in bfloat16 or wider, within the bound.
A program may use at most 128 MiB of HBM per device.

```python
import math
import jax
import jax.numpy as jnp
from jax import lax

GRID = 128
FIELDS = 8
CH = 64
MODES = 16
SAMPLES = 8


def block_levels(own_key, dims, split, smallest, largest):
    gain, own = 1.0, jax.random.fold_in(own_key, 6)
    for position, shards_of in split:
        heights = jnp.exp(jax.random.uniform(jax.random.fold_in(own, position), (shards_of,), jnp.float32, smallest / len(split), largest / len(split)))
        gain = gain * jnp.repeat(heights, dims[position] // shards_of).reshape([-1 if axis == position else 1 for axis in range(len(dims))])
    return gain


def centred(rng, extent, scale, most, pieces=(), held_as=jnp.bfloat16):
    drawn = scale * jax.random.normal(rng, extent, jnp.float32)
    if pieces:
        drawn = drawn * block_levels(rng, extent, pieces, -0.22, 0.18)
    return jnp.clip(drawn, -most, most).astype(held_as)


def setup_inputs(seed: int = 0) -> dict:
    seeds = jax.random.split(jax.random.key(seed), 7)
    fields = centred(seeds[0], (SAMPLES, FIELDS, GRID, GRID, GRID), 1.0, 6.0, ((0, 4), (2, 64)))
    lift_weight = centred(seeds[1], (FIELDS, CH), FIELDS ** -0.5, 2.0)
    mode_weight = centred(seeds[2], (MODES, MODES * MODES, CH, CH), CH ** -0.5, 0.75, ((1, 64),))
    local_weight = centred(seeds[3], (CH, CH), CH ** -0.5, 0.75)
    project_weight = centred(seeds[4], (CH, FIELDS), CH ** -0.5, 0.75)
    out_cotangent = centred(seeds[5], (SAMPLES, FIELDS, GRID, GRID, GRID), 1.0, 6.0, ((0, 4), (2, 64)))
    return dict(fields=fields, lift_weight=lift_weight, mode_weight=mode_weight, local_weight=local_weight, project_weight=project_weight, out_cotangent=out_cotangent)


def basis(count, length, start, rows, scale):
    index = start + jnp.arange(rows, dtype=jnp.int32)
    order = jnp.arange(count, dtype=jnp.int32)
    freq = (order + 1) // 2
    phase = freq[:, None] * index[None, :] % length
    angle = phase.astype(jnp.float32) * (2.0 * math.pi / length)
    wave = jnp.where((order % 2 == 0)[:, None], jnp.cos(angle), jnp.sin(angle))
    return wave * scale

def to_half(value):
    return lax.optimization_barrier(value.astype(jnp.bfloat16)).astype(jnp.float32)

def product(form, left, right):
    return jnp.einsum(form, left, right, precision=lax.Precision.HIGHEST)

def analyze(field, table_y, table_z, table_x):
    part = to_half(product('cxyz,ky->cxkz', field, table_y))
    part = to_half(product('cxkz,jz->cxkj', part, table_z))
    part = part.reshape(part.shape[0], part.shape[1], -1)
    return to_half(product('cxm,kx->kmc', part, table_x))

def synthesize(coef, table_x, table_z, table_y):
    planes = product('kmd,kx->dxm', coef, table_x)
    planes = planes.reshape(planes.shape[0], planes.shape[1], MODES, MODES)
    inner = to_half(product('dxab,bz->dxaz', planes, table_z))
    return product('dxaz,ay->dxyz', inner, table_y)

def slope(value):
    normal = 0.5 * (1.0 + lax.erf(value * (1.0 / math.sqrt(2.0))))
    density = jnp.exp(-0.5 * value * value) * (1.0 / math.sqrt(2.0 * math.pi))
    return normal + value * density

def reference(fields, lift_weight, mode_weight, local_weight, project_weight, out_cotangent):
    ana_full = basis(MODES, GRID, 0, GRID, math.sqrt(2.0 / GRID))
    syn_full = basis(MODES, GRID, 0, GRID, math.sqrt(2.0 / MODES))
    ana_half = to_half(ana_full)
    syn_half = to_half(syn_full)
    lift_wide = lift_weight.astype(jnp.float32)
    mode_wide = mode_weight.astype(jnp.float32)
    local_wide = local_weight.astype(jnp.float32)
    project_wide = project_weight.astype(jnp.float32)

    def one_sample(grad_total, pair):
        sample, cotangent = pair
        lifted = to_half(product('fxyz,fc->cxyz', sample.astype(jnp.float32), lift_wide))
        coef = analyze(lifted, ana_half, ana_half, ana_half)
        mixed = to_half(product('kmc,kmcd->kmd', coef, mode_wide))
        spectral = synthesize(mixed, syn_half, syn_full, syn_half)
        pre = product('cxyz,cd->dxyz', lifted, local_wide) + spectral
        hidden = to_half(jax.nn.gelu(pre, approximate=False))
        prediction = product('cxyz,cf->fxyz', hidden, project_wide).astype(jnp.bfloat16)
        back_hidden = product('fxyz,cf->cxyz', cotangent.astype(jnp.float32), project_wide)
        grad_pre = to_half(back_hidden * slope(pre))
        coef_grad = analyze(grad_pre, syn_half, syn_half, syn_half)
        grad_total = grad_total + product('kmc,kmd->kmcd', coef, coef_grad)
        back_coef = to_half(product('kmd,kmcd->kmc', coef_grad, mode_wide))
        back_spec = synthesize(back_coef, ana_half, ana_full, ana_half)
        grad_lift = to_half(product('dxyz,cd->cxyz', grad_pre, local_wide) + back_spec)
        field_grad = product('cxyz,fc->fxyz', grad_lift, lift_wide).astype(jnp.bfloat16)
        return (grad_total, (prediction, field_grad))
    start_grad = jnp.zeros(mode_weight.shape, jnp.float32)
    mode_grad, (prediction, field_grad) = lax.scan(one_sample, start_grad, (fields, out_cotangent))
    return (prediction, mode_grad, field_grad)
```

```python
import math

import jax
import jax.numpy as jnp
from jax import lax
from jax.sharding import PartitionSpec as P

F32 = jnp.float32
BF = jnp.bfloat16


def basis(count, length, start, rows, scale):
    index = start + jnp.arange(rows, dtype=jnp.int32)
    order = jnp.arange(count, dtype=jnp.int32)
    freq = (order + 1) // 2
    phase = freq[:, None] * index[None, :] % length
    angle = phase.astype(jnp.float32) * (2.0 * math.pi / length)
    wave = jnp.where((order % 2 == 0)[:, None], jnp.cos(angle), jnp.sin(angle))
    return wave * scale


def slope(value):
    normal = 0.5 * (1.0 + lax.erf(value * (1.0 / math.sqrt(2.0))))
    density = jnp.exp(-0.5 * value * value) * (1.0 / math.sqrt(2.0 * math.pi))
    return normal + value * density


def ein(form, left, right):
    return jnp.einsum(form, left, right, preferred_element_type=F32)


def analyze(field, half):
    samples, width, slab, size, _ = field.shape
    modes = half.shape[0]
    part = ein("scxyz,ky->scxkz", field, half).astype(BF)
    part = ein("scxkz,jz->scxkj", part, half).astype(BF)
    part = part.reshape(samples, width, slab, modes * modes)
    moved = lax.all_to_all(part, "space", split_axis=3, concat_axis=2, tiled=True)
    return ein("scxm,kx->skmc", moved, half)


def synthesize(coef, half):
    samples, modes, share, width = coef.shape
    planes = ein("skmd,kx->sdxm", coef, half).astype(BF)
    planes = lax.all_to_all(planes, "space", split_axis=2, concat_axis=3, tiled=True)
    planes = planes.reshape(samples, width, planes.shape[2], modes, modes)
    inner = ein("sdxab,bz->sdxaz", planes, half).astype(BF)
    return ein("sdxaz,ay->sdxyz", inner, half)


def local(fields, lift_weight, mode_weight, local_weight, project_weight, out_cotangent):
    size = fields.shape[3]
    modes = mode_weight.shape[0]
    ana = basis(modes, size, 0, size, math.sqrt(2.0 / size)).astype(BF)
    syn = basis(modes, size, 0, size, math.sqrt(2.0 / modes)).astype(BF)
    both = ein("fc,cd->fd", lift_weight, local_weight).astype(BF)
    coef_field = analyze(fields, ana).astype(BF)
    coef = ein("skmf,fc->skmc", coef_field, lift_weight).astype(BF)
    mixed = ein("skmc,kmcd->skmd", coef, mode_weight).astype(BF)
    pre = ein("sfxyz,fd->sdxyz", fields, both) + synthesize(mixed, syn)
    hidden = jax.nn.gelu(pre, approximate=False).astype(BF)
    prediction = ein("scxyz,cf->sfxyz", hidden, project_weight).astype(BF)
    back_hidden = ein("sfxyz,cf->scxyz", out_cotangent, project_weight)
    grad_pre = (back_hidden * slope(pre)).astype(BF)
    coef_grad = analyze(grad_pre, syn).astype(BF)
    local_grad = ein("skmc,skmd->kmcd", coef, coef_grad)
    mode_grad = lax.psum(local_grad.astype(BF), "dp").astype(F32)
    back_coef = ein("skmd,kmcd->skmc", coef_grad, mode_weight).astype(BF)
    back_field = ein("skmc,fc->skmf", back_coef, lift_weight).astype(BF)
    field_grad = (ein("sdxyz,fd->sfxyz", grad_pre, both) + synthesize(back_field, ana)).astype(BF)
    return (prediction, mode_grad, field_grad)


def solution(mesh):
    wide = P("dp", None, "space", None, None)
    return jax.shard_map(
        local,
        mesh=mesh,
        in_specs=(wide, P(), P(None, "space", None, None), P(), P(), wide),
        out_specs=(wide, P(None, "space", None, None), wide),
        check_vma=False,
    )
```

```python
import functools
import math

import jax
import jax.numpy as jnp
import ml_dtypes
import numpy as np
from jax import lax
from jax.experimental import pallas as pl
from jax.experimental.pallas import tpu as pltpu
from jax.sharding import PartitionSpec as P

F32 = jnp.float32
BF = jnp.bfloat16
MESH = pl.DeviceIdType.MESH

GRID = 128
FIELDS = 8
CH = 64
MODES = 16
PIX = GRID * GRID
ROWS = 32
TILE = 512
ANA = 1.0 / 512.0
SYN = 8.0 ** -1.5


def dot(a, b, dims=((1,), (0,))):
    return lax.dot_general(a, b, (dims, ((), ())), preferred_element_type=F32)


def waves():
    order = np.arange(MODES)
    angle = 2.0 * np.pi * ((order[:, None] + 1) // 2 * np.arange(GRID)[None, :] % GRID) / GRID
    return np.where((order % 2 == 0)[:, None], np.cos(angle), np.sin(angle))


def half(x):
    return np.asarray(x, np.float32).astype(ml_dtypes.bfloat16)


def tables(space):
    w = waves()
    share = MODES * MODES // space
    row = np.arange(MODES * MODES)
    mode = share * (row % space) + row // space
    grid = (w[mode // MODES][:, :, None] * w[mode % MODES][:, None, :]).reshape(MODES * MODES, PIX)
    a0, a1 = w[:, 0::2], w[:, 1::2]
    rep0 = np.repeat(a0, 8, axis=0)
    rep1 = np.repeat(a1, 8, axis=0)
    eye = np.eye(8)
    kron = np.concatenate([np.kron(a0, eye), np.kron(a1, eye)], axis=0)
    return half(grid), half(rep0), half(rep1), half(rep0.T), half(rep1.T), half(kron), half(kron.T)


def iota(shape, axis):
    return lax.broadcasted_iota(jnp.int32, shape, axis)


def activation(v, back):
    size = jnp.abs(v)
    t = 1.0 / (1.0 + (0.3275911 / math.sqrt(2.0)) * size)
    e = jnp.exp2((v * v) * (-0.5 / math.log(2.0)))
    poly = 0.5 * 1.061405429
    for c in (-1.453152027, 1.421413741, -0.284496736, 0.254829592):
        poly = poly * t + 0.5 * c
    tail = poly * t * e
    normal = jnp.where(v >= 0.0, 1.0 - tail, tail)
    hidden = v * normal
    grad = back * (normal + v * (e * (1.0 / math.sqrt(2.0 * math.pi))))
    return hidden, grad


def exchange(src, dst, send_sem, recv_sem, me, space):
    def body(step, carry):
        to = lax.rem(me + step, space)
        pltpu.make_async_remote_copy(
            src_ref=src.at[to],
            dst_ref=dst.at[me],
            send_sem=send_sem,
            recv_sem=recv_sem,
            device_id={"space": to},
            device_id_type=MESH,
        ).start()
        return carry

    lax.fori_loop(1, space, body, 0)
    dst[me] = src[me]


def arrive(src, dst, send_sem, recv_sem, me, space):
    whole = pltpu.make_async_remote_copy(
        src_ref=src.at[pl.ds(0, space - 1)],
        dst_ref=dst.at[pl.ds(0, space - 1)],
        send_sem=send_sem,
        recv_sem=recv_sem,
        device_id={"space": lax.rem(me + 1, space)},
        device_id_type=MESH,
    )
    whole.wait_send()
    whole.wait_recv()


def kernel(
    space, dp,
    f_hbm, c_hbm, w_hbm, t_hbm, lift_ref, local_ref, project_ref,
    rep0_ref, rep1_ref, rep0t_ref, rep1t_ref, kron_ref, kront_ref,
    pred_hbm, mode_hbm, field_hbm,
    t_ref, w_ref, raw_f, raw_c, wide, flat_f, flat_c, part, out_p, out_f, mode_out,
    pre_s, back_s, hid_s, grad_s, acc, planes, rows_s, stack,
    send1, recv1, send2, recv2, send3, recv3, send4, recv4, team, team_w,
    load_sem, store_sem, send_sem, recv_sem,
):
    me = lax.axis_index("space")
    my_dp = lax.axis_index("dp")
    share = MODES * MODES // space
    chunks = 8
    width = PIX // chunks

    load_f = pltpu.make_async_copy(f_hbm, raw_f, load_sem.at[0])
    load_f.start()
    load_t = []
    for n in range(chunks):
        cut = pl.ds(n * width, width)
        load_t.append(pltpu.make_async_copy(t_hbm.at[:, cut], t_ref.at[:, cut], load_sem.at[3 + n]))
        load_t[-1].start()
    load_c = pltpu.make_async_copy(c_hbm, raw_c, load_sem.at[1])
    load_c.start()
    load_w = pltpu.make_async_copy(w_hbm, w_ref, load_sem.at[2])
    load_w.start()

    barrier = pltpu.get_barrier_semaphore()

    def greet(step, carry):
        pl.semaphore_signal(barrier, inc=1, device_id={"space": lax.rem(me + step, space)}, device_id_type=MESH)
        return carry

    lax.fori_loop(1, space, greet, 0)
    for step in range(1, dp):
        pl.semaphore_signal(barrier, inc=1, device_id={"dp": lax.rem(my_dp + step, dp)}, device_id_type=MESH)

    lift = lift_ref[...]
    pick32 = (iota((ROWS, FIELDS), 0) // 2 % FIELDS == iota((ROWS, FIELDS), 1)).astype(F32).astype(BF)
    pick128 = (iota((128, FIELDS), 0) // 2 % FIELDS == iota((128, FIELDS), 1)).astype(F32).astype(BF)
    p_row, q_lane = iota((ROWS, 256), 0), iota((ROWS, 256), 1)
    same = (p_row // 16 == q_lane // 128) & (p_row % 2 == q_lane // CH % 2)
    both = dot(lift, local_ref[...]).astype(BF)
    both32 = dot(pick32, both)
    both32 = jnp.where(same, jnp.concatenate([both32] * 4, axis=1), 0.0)
    proj32 = dot(pick32, project_ref[...])
    proj32 = jnp.where(same, jnp.concatenate([proj32] * 4, axis=1), 0.0)
    down_field = both32.astype(BF)
    down_proj = proj32.astype(BF)
    up_field = both32.T.astype(BF)
    up_proj = proj32.T.astype(BF)
    lift128 = dot(pick128, lift)
    lift_big = jnp.concatenate([lift128] * 4, axis=1)
    lift_bigt = lift_big.T.astype(BF)
    lift_big = lift_big.astype(BF)
    r128, l128 = iota((128, 128), 0), iota((128, 128), 1)
    mask_field = (r128 % 4 == l128 // 32) & (r128 // 4 % 2 == l128 // 16 % 2)
    first_plane = l128 % 2 == 0
    r256, l256 = iota((128, 256), 0), iota((128, 256), 1)
    mask_mode = r256 % 4 == l256 // CH

    def relayout(raw, flat):
        def widen(n, carry):
            cut = pl.ds(n * 4, 4)
            wide[pl.ds(pl.multiple_of(n * 512, 512), 512), :] = raw[cut].astype(F32).reshape(512, 128)
            return carry

        lax.fori_loop(0, 8, widen, 0)

        def turn(n, carry):
            for u in range(8):
                y = n * 8 + u
                rows = wide[pl.ds(y, ROWS, stride=GRID), :]
                flat[:, pl.ds(pl.multiple_of(y * GRID, GRID), GRID)] = rows.astype(BF)
            return carry

        lax.fori_loop(0, GRID // 8, turn, 0)

    load_f.wait()
    relayout(raw_f, flat_f)
    spec = None
    for n in range(chunks):
        load_t[n].wait()
        cut = pl.ds(n * width, width)
        term = dot(t_ref[:, cut], flat_f[:, cut], ((1,), (1,)))
        spec = term if spec is None else spec + term
    send1[...] = jnp.concatenate([spec[b * space:(b + 1) * space] for b in range(share)], axis=1).reshape(space, 1, 128)

    pl.semaphore_wait(barrier, space - 1 + dp - 1)
    exchange(send1, recv1, send_sem.at[0], recv_sem.at[0], me, space)
    load_c.wait()
    relayout(raw_c, flat_c)
    load_w.wait()
    arrive(send1, recv1, send_sem.at[0], recv_sem.at[0], me, space)

    got = recv1[...].reshape(space, 128).astype(BF)
    coef = jnp.where(first_plane, dot(rep0_ref[...], got), dot(rep1_ref[...], got)) * ANA
    coef = jnp.where(mask_field, coef, 0.0).astype(BF)
    coef = dot(coef, lift_big)
    team_w[:, 0:CH] = coef[:, 0:CH]
    stack[...] = jnp.where(mask_mode, coef, 0.0)
    mixed = []
    for k in range(MODES):
        mixed.append(dot(stack[k * 8:k * 8 + 8, :].astype(BF), w_ref[k]))
    mixed = (jnp.concatenate(mixed, axis=0) * SYN).astype(BF)
    out = jnp.concatenate(
        [dot(kront_ref[:, 0:128], mixed), dot(kront_ref[:, 128:256], mixed)], axis=1
    )
    send2[...] = out.reshape(space, 8, 128).astype(BF)
    exchange(send2, recv2, send_sem.at[1], recv_sem.at[1], me, space)
    acc[...] = jnp.zeros_like(acc)
    arrive(send2, recv2, send_sem.at[1], recv_sem.at[1], me, space)

    rows_s[...] = recv2[...].astype(F32).reshape(space * 8, 128)
    for s in range(2):
        for b in range(share):
            block = rows_s[pl.ds(s * 4 + b, space, stride=8), :]
            planes[s * 128:(s + 1) * 128, b * space:(b + 1) * space] = block.T.astype(BF)

    def tile(n, carry):
        cut = pl.ds(pl.multiple_of(n * TILE, TILE), TILE)
        pre_s[...] = dot(planes[...], t_ref[:, cut]) + dot(up_field, flat_f[:, cut])
        back_s[...] = dot(up_proj, flat_c[:, cut])
        for r in range(0, 256, 16):
            hidden, grad = activation(pre_s[r:r + 16, :], back_s[r:r + 16, :])
            hid_s[r:r + 16, :] = hidden.astype(BF)
            grad_s[r:r + 16, :] = grad.astype(BF)
        guess = dot(down_proj, hid_s[...])
        local = dot(down_field, grad_s[...])
        for u in range(TILE // GRID):
            y = n * (TILE // GRID) + u
            wide[pl.ds(y, ROWS, stride=GRID), :] = guess[:, u * GRID:(u + 1) * GRID]
            part[pl.ds(y, ROWS, stride=GRID), :] = local[:, u * GRID:(u + 1) * GRID]
        acc[...] += dot(t_ref[:, cut], grad_s[...], ((1,), (1,)))
        return carry

    lax.fori_loop(0, PIX // TILE, tile, 0)

    for s in range(2):
        for b in range(share):
            rows_s[pl.ds(s * 4 + b, space, stride=8), :] = acc[b * space:(b + 1) * space, s * 128:(s + 1) * 128]
    send3[...] = rows_s[...].reshape(space, 8, 128).astype(BF)
    exchange(send3, recv3, send_sem.at[2], recv_sem.at[2], me, space)

    def narrow(src, dst):
        def body(n, carry):
            dst[pl.ds(n * 4, 4)] = src[pl.ds(pl.multiple_of(n * 512, 512), 512), :].reshape(4, 128, 128).astype(BF)
            return carry

        lax.fori_loop(0, 8, body, 0)

    narrow(wide, out_p)
    store_p = pltpu.make_async_copy(out_p, pred_hbm, store_sem.at[0])
    store_p.start()
    arrive(send3, recv3, send_sem.at[2], recv_sem.at[2], me, space)

    got = recv3[...].astype(F32).reshape(space * 8, 128).astype(BF)
    full = dot(kron_ref[...], got)
    cgrad = (full[0:128, 0:CH] + full[128:256, CH:128]) * SYN
    team_w[:, CH:128] = cgrad
    back = []
    for k in range(MODES):
        back.append(dot(cgrad[k * 8:k * 8 + 8, :].astype(BF), w_ref[k], ((1,), (1,))))
    back = jnp.where(mask_mode, jnp.concatenate(back, axis=0), 0.0).astype(BF)
    back = jnp.where(mask_field, dot(back, lift_bigt) * ANA, 0.0).astype(BF)
    lanes = iota((space, 128), 1)
    out = jnp.where(lanes % 2 == 0, dot(rep0t_ref[...], back), dot(rep1t_ref[...], back))
    send4[...] = out.reshape(space, 1, 128)
    exchange(send4, recv4, send_sem.at[3], recv_sem.at[3], me, space)

    team[my_dp] = team_w[...].astype(BF)
    copies = []
    for step in range(1, dp):
        copies.append(pltpu.make_async_remote_copy(
            src_ref=team.at[my_dp],
            dst_ref=team.at[my_dp],
            send_sem=send_sem.at[3 + step],
            recv_sem=recv_sem.at[3 + step],
            device_id={"dp": lax.rem(my_dp + step, dp)},
            device_id_type=MESH,
        ))
        copies[-1].start()
    for copy in copies:
        copy.wait()
    m_row, m_lane = iota((32, 256), 0), iota((32, 256), 1)
    mask_team = m_row % 4 == m_lane // CH
    for k in range(MODES):
        rows = jnp.concatenate([team[d].astype(F32)[k * 8:k * 8 + 8, :] for d in range(dp)], axis=0)
        left = jnp.where(mask_team, jnp.concatenate([rows[:, 0:CH]] * 4, axis=1), 0.0)
        mode_out[k] = dot(left.T.astype(BF), rows[:, CH:128].astype(BF))
    store_m = pltpu.make_async_copy(mode_out, mode_hbm, store_sem.at[1])
    store_m.start()
    arrive(send4, recv4, send_sem.at[3], recv_sem.at[3], me, space)

    turned = recv4[...].reshape(space, 128).T
    field = jnp.concatenate([turned[b * 32:(b + 1) * 32] for b in range(share)], axis=1).astype(BF)

    def last(n, carry):
        cut = pl.ds(pl.multiple_of(n * TILE, TILE), TILE)
        value = dot(field, t_ref[:, cut])
        for u in range(TILE // GRID):
            at = pl.ds(n * (TILE // GRID) + u, ROWS, stride=GRID)
            part[at, :] = part[at, :] + value[:, u * GRID:(u + 1) * GRID]
        return carry

    lax.fori_loop(0, PIX // TILE, last, 0)
    narrow(part, out_f)
    store_f = pltpu.make_async_copy(out_f, field_hbm, store_sem.at[2])
    store_f.start()
    store_p.wait()
    store_m.wait()
    store_f.wait()


def solution(mesh):
    space, dp = mesh.shape["space"], mesh.shape["dp"]
    consts = tables(space)

    def local(fields, lift_weight, mode_weight, local_weight, project_weight, out_cotangent):
        planes = (ROWS, GRID, GRID)
        hbm = pl.BlockSpec(memory_space=pl.ANY)
        vmem = pl.BlockSpec(memory_space=pltpu.VMEM)
        share = MODES * MODES // space
        prediction, mode_grad, field_grad = pl.pallas_call(
            functools.partial(kernel, space, dp),
            out_shape=(
                jax.ShapeDtypeStruct(planes, BF),
                jax.ShapeDtypeStruct((MODES, share * CH, CH), F32),
                jax.ShapeDtypeStruct(planes, BF),
            ),
            in_specs=[hbm] * 4 + [vmem] * 9,
            out_specs=(hbm, hbm, hbm),
            scratch_shapes=[
                pltpu.VMEM((256, PIX), BF),
                pltpu.VMEM((MODES, share * CH, CH), BF),
                pltpu.VMEM(planes, BF),
                pltpu.VMEM(planes, BF),
                pltpu.VMEM((ROWS * GRID, GRID), F32),
                pltpu.VMEM((ROWS, PIX), BF),
                pltpu.VMEM((ROWS, PIX), BF),
                pltpu.VMEM((ROWS * GRID, GRID), F32),
                pltpu.VMEM(planes, BF),
                pltpu.VMEM(planes, BF),
                pltpu.VMEM((MODES, share * CH, CH), F32),
                pltpu.VMEM((256, TILE), F32),
                pltpu.VMEM((256, TILE), F32),
                pltpu.VMEM((256, TILE), BF),
                pltpu.VMEM((256, TILE), BF),
                pltpu.VMEM((256, 256), F32),
                pltpu.VMEM((256, 256), BF),
                pltpu.VMEM((space * 8, 128), F32),
                pltpu.VMEM((128, 256), F32),
                pltpu.VMEM((space, 1, 128), F32),
                pltpu.VMEM((space, 1, 128), F32),
                pltpu.VMEM((space, 8, 128), BF),
                pltpu.VMEM((space, 8, 128), BF),
                pltpu.VMEM((space, 8, 128), BF),
                pltpu.VMEM((space, 8, 128), BF),
                pltpu.VMEM((space, 1, 128), F32),
                pltpu.VMEM((space, 1, 128), F32),
                pltpu.VMEM((dp, 128, 128), BF),
                pltpu.VMEM((128, 128), F32),
                pltpu.SemaphoreType.DMA((11,)),
                pltpu.SemaphoreType.DMA((3,)),
                pltpu.SemaphoreType.DMA((3 + dp,)),
                pltpu.SemaphoreType.DMA((3 + dp,)),
            ],
            compiler_params=pltpu.CompilerParams(
                collective_id=0, has_side_effects=True, vmem_limit_bytes=56 * 1024 * 1024
            ),
        )(
            fields.reshape(planes),
            out_cotangent.reshape(planes),
            mode_weight.reshape(MODES, share * CH, CH),
            jnp.asarray(consts[0]),
            lift_weight,
            local_weight,
            project_weight.T,
            *[jnp.asarray(c) for c in consts[1:]],
        )
        return (
            prediction.reshape(fields.shape),
            mode_grad.reshape(mode_weight.shape),
            field_grad.reshape(fields.shape),
        )

    wide = P("dp", None, "space", None, None)
    return jax.shard_map(
        local,
        mesh=mesh,
        in_specs=(wide, P(), P(None, "space", None, None), P(), P(), wide),
        out_specs=(wide, P(None, "space", None, None), wide),
        check_vma=False,
    )
```

```python
import functools
import math

import jax
import jax.numpy as jnp
import ml_dtypes
import numpy as np
from jax import lax
from jax.experimental import pallas as pl
from jax.experimental.pallas import tpu as pltpu
from jax.sharding import PartitionSpec as P

F32 = jnp.float32
BF = jnp.bfloat16
MESH = pl.DeviceIdType.MESH

GRID = 128
FIELDS = 8
CH = 64
MODES = 16
PIX = GRID * GRID
ROWS = 32
TILE = 1024
ANA = 1.0 / 512.0
SYN = 8.0 ** -1.5


def dot(a, b, dims=((1,), (0,))):
    return lax.dot_general(a, b, (dims, ((), ())), preferred_element_type=F32)


def waves():
    order = np.arange(MODES)
    angle = 2.0 * np.pi * ((order[:, None] + 1) // 2 * np.arange(GRID)[None, :] % GRID) / GRID
    return np.where((order % 2 == 0)[:, None], np.cos(angle), np.sin(angle))


def half(x):
    return np.asarray(x, np.float32).astype(ml_dtypes.bfloat16)


def tables(space):
    w = waves()
    share = MODES * MODES // space
    row = np.arange(MODES * MODES)
    mode = share * (row % space) + row // space
    grid = (w[mode // MODES][:, :, None] * w[mode % MODES][:, None, :]).reshape(MODES * MODES, PIX)
    a0, a1 = w[:, 0::2], w[:, 1::2]
    rep0 = np.repeat(a0, 8, axis=0)
    rep1 = np.repeat(a1, 8, axis=0)
    eye = np.eye(8)
    wave_z = w[mode % MODES]
    pair_y = np.kron(np.eye(2), w)
    kron = np.concatenate([np.kron(a0, eye), np.kron(a1, eye)], axis=0)
    return half(grid), half(rep0), half(rep1), half(rep0.T), half(rep1.T), half(kron), half(kron.T), half(wave_z), half(pair_y), half(pair_y.T)


def iota(shape, axis):
    return lax.broadcasted_iota(jnp.int32, shape, axis)


def activation(v, back):
    normal = 0.5 + 0.5 * lax.erf(v * math.sqrt(0.5))
    e = jnp.exp2((v * v) * (-0.5 / math.log(2.0)))
    grad = back * (normal + v * (e * (1.0 / math.sqrt(2.0 * math.pi))))
    return v * normal, grad


def hops(step):
    x, z, y = step
    return min(x, 4 - x) + min(z, 8 - z) + y


STEPS = sorted(
    [(x, z, y) for x in range(4) for z in range(8) for y in range(2) if x or z or y],
    key=hops, reverse=True,
)


def exchange(src, dst, send_sem, recv_sem, me, space):
    x, z, y = me // 16, me // 2 % 8, me % 2
    for dx, dz, dy in STEPS:
        to = lax.rem(x + dx, 4) * 16 + lax.rem(z + dz, 8) * 2 + lax.rem(y + dy, 2)
        pltpu.make_async_remote_copy(
            src_ref=src.at[to],
            dst_ref=dst.at[me],
            send_sem=send_sem,
            recv_sem=recv_sem,
            device_id={"space": to},
            device_id_type=MESH,
        ).start()
    dst[me] = src[me]


def arrive(src, dst, send_sem, recv_sem, me, space):
    whole = pltpu.make_async_remote_copy(
        src_ref=src.at[pl.ds(0, space - 1)],
        dst_ref=dst.at[pl.ds(0, space - 1)],
        send_sem=send_sem,
        recv_sem=recv_sem,
        device_id={"space": lax.rem(me + 1, space)},
        device_id_type=MESH,
    )
    whole.wait_send()
    whole.wait_recv()


def kernel(
    space, dp,
    f_hbm, c_hbm, w_hbm, t_hbm, lift_ref, local_ref, project_ref,
    rep0_ref, rep1_ref, rep0t_ref, rep1t_ref, kron_ref, kront_ref, wavez_ref, pairy_ref,
    pred_hbm, part_hbm, last_ref, team_ref,
    t_ref, w_ref, raw_f, raw_c, wide, flat_f, flat_c, part, out_p, out_f, part_y,
    pre_a, back_a, hid_a, grad_a, pre_b, back_b, hid_b, grad_b, acc, planes, rows_s, stack,
    send1, recv1, send2, recv2, send3, recv3, send4, recv4, team, team_w,
    load_sem, store_sem, send_sem, recv_sem,
):
    me = lax.axis_index("space")
    my_dp = lax.axis_index("dp")
    share = MODES * MODES // space
    chunks = 8
    width = PIX // chunks

    load_f = pltpu.make_async_copy(f_hbm, raw_f, load_sem.at[0])
    load_f.start()
    load_t = []
    for n in range(chunks):
        cut = pl.ds(n * width, width)
        load_t.append(pltpu.make_async_copy(t_hbm.at[:, cut], t_ref.at[:, cut], load_sem.at[3 + n]))
        load_t[-1].start()
    load_c = pltpu.make_async_copy(c_hbm, raw_c, load_sem.at[1])
    load_c.start()
    load_w = pltpu.make_async_copy(w_hbm, w_ref, load_sem.at[2])
    load_w.start()

    barrier = pltpu.get_barrier_semaphore()

    def greet(step, carry):
        pl.semaphore_signal(barrier, inc=1, device_id={"space": lax.rem(me + step, space)}, device_id_type=MESH)
        return carry

    lax.fori_loop(1, space, greet, 0)
    for step in range(1, dp):
        pl.semaphore_signal(barrier, inc=1, device_id={"dp": lax.rem(my_dp + step, dp)}, device_id_type=MESH)

    lift = lift_ref[...]
    pick32 = (iota((ROWS, FIELDS), 0) // 2 % FIELDS == iota((ROWS, FIELDS), 1)).astype(F32).astype(BF)
    pick128 = (iota((128, FIELDS), 0) // 2 % FIELDS == iota((128, FIELDS), 1)).astype(F32).astype(BF)
    p_row, q_lane = iota((ROWS, 256), 0), iota((ROWS, 256), 1)
    same = (p_row // 16 == q_lane // 128) & (p_row % 2 == q_lane // CH % 2)
    both = dot(lift, local_ref[...]).astype(BF)
    both32 = dot(pick32, both)
    both32 = jnp.where(same, jnp.concatenate([both32] * 4, axis=1), 0.0)
    proj32 = dot(pick32, project_ref[...])
    proj32 = jnp.where(same, jnp.concatenate([proj32] * 4, axis=1), 0.0)
    down_field = both32.astype(BF)
    down_proj = proj32.astype(BF)
    up_field = both32.T.astype(BF)
    up_proj = proj32.T.astype(BF)
    lift128 = dot(pick128, lift)
    lift_big = jnp.concatenate([lift128] * 4, axis=1)
    lift_bigt = lift_big.T.astype(BF)
    lift_big = lift_big.astype(BF)
    r128, l128 = iota((128, 128), 0), iota((128, 128), 1)
    mask_field = (r128 % 4 == l128 // 32) & (r128 // 4 % 2 == l128 // 16 % 2)
    first_plane = l128 % 2 == 0
    r256, l256 = iota((128, 256), 0), iota((128, 256), 1)
    mask_mode = r256 % 4 == l256 // CH

    def relayout(raw, flat):
        def widen(n, carry):
            cut = pl.ds(n * 4, 4)
            wide[pl.ds(pl.multiple_of(n * 512, 512), 512), :] = raw[cut].astype(F32).reshape(512, 128)
            return carry

        lax.fori_loop(0, 8, widen, 0)

        def turn(n, carry):
            for u in range(8):
                y = n * 8 + u
                rows = wide[pl.ds(y, ROWS, stride=GRID), :]
                flat[:, pl.ds(pl.multiple_of(y * GRID, GRID), GRID)] = rows.astype(BF)
            return carry

        lax.fori_loop(0, GRID // 8, turn, 0)

    load_f.wait()
    for n in range(ROWS // 2):
        pair = raw_f[2 * n:2 * n + 2].reshape(2 * GRID, GRID)
        part_y[n * 32:n * 32 + 32, :] = dot(pairy_ref[...], pair).astype(BF)
    value = dot(part_y[...], wavez_ref[...], ((1,), (1,)))
    s_row, s_lane = iota((512, 256), 0), iota((512, 256), 1)
    value = jnp.where(s_row % MODES == s_lane % space // share, value, 0.0).astype(BF)
    fold = (iota((ROWS, 512), 0) == iota((ROWS, 512), 1) // MODES).astype(F32).astype(BF)
    spec = dot(fold, value).T
    send1[...] = jnp.concatenate([spec[b * space:(b + 1) * space] for b in range(share)], axis=1).reshape(space, 1, 128)

    pl.semaphore_wait(barrier, space - 1 + dp - 1)
    exchange(send1, recv1, send_sem.at[0], recv_sem.at[0], me, space)
    relayout(raw_f, flat_f)
    load_c.wait()
    relayout(raw_c, flat_c)
    load_w.wait()
    arrive(send1, recv1, send_sem.at[0], recv_sem.at[0], me, space)

    got = recv1[...].reshape(space, 128).astype(BF)
    coef = jnp.where(first_plane, dot(rep0_ref[...], got), dot(rep1_ref[...], got)) * ANA
    coef = jnp.where(mask_field, coef, 0.0).astype(BF)
    coef = dot(coef, lift_big)
    team_w[:, 0:CH] = coef[:, 0:CH]
    stack[...] = jnp.where(mask_mode, coef, 0.0)
    mixed = []
    for k in range(MODES):
        mixed.append(dot(stack[k * 8:k * 8 + 8, :].astype(BF), w_ref[k]))
    mixed = (jnp.concatenate(mixed, axis=0) * SYN).astype(BF)
    out = jnp.concatenate(
        [dot(kront_ref[:, 0:128], mixed), dot(kront_ref[:, 128:256], mixed)], axis=1
    )
    send2[...] = out.reshape(space, 8, 128).astype(BF)
    exchange(send2, recv2, send_sem.at[1], recv_sem.at[1], me, space)
    acc[...] = jnp.zeros_like(acc)
    for copy in load_t:
        copy.wait()
    arrive(send2, recv2, send_sem.at[1], recv_sem.at[1], me, space)

    rows_s[...] = recv2[...].astype(F32).reshape(space * 8, 128)
    for s in range(2):
        for b in range(share):
            block = rows_s[pl.ds(s * 4 + b, space, stride=8), :]
            planes[s * 128:(s + 1) * 128, b * space:(b + 1) * space] = block.T.astype(BF)

    def front(n, pre_s, back_s):
        cut = pl.ds(pl.multiple_of(n * TILE, TILE), TILE)
        pre_s[...] = dot(planes[...], t_ref[:, cut]) + dot(up_field, flat_f[:, cut])
        back_s[...] = dot(up_proj, flat_c[:, cut])

    def middle(pre_s, back_s, hid_s, grad_s):
        for r in range(0, 256, 16):
            for c in range(0, TILE, 256):
                at = (slice(r, r + 16), slice(c, c + 256))
                hidden, grad = activation(pre_s[at], back_s[at])
                hid_s[at] = hidden.astype(BF)
                grad_s[at] = grad.astype(BF)

    def back(n, hid_s, grad_s):
        cut = pl.ds(pl.multiple_of(n * TILE, TILE), TILE)
        guess = dot(down_proj, hid_s[...])
        local = dot(down_field, grad_s[...])
        for u in range(TILE // GRID):
            y = n * (TILE // GRID) + u
            wide[pl.ds(y, ROWS, stride=GRID), :] = guess[:, u * GRID:(u + 1) * GRID]
            part[pl.ds(y, ROWS, stride=GRID), :] = local[:, u * GRID:(u + 1) * GRID]
        acc[...] += dot(t_ref[:, cut], grad_s[...], ((1,), (1,)))

    tiles = PIX // TILE
    front(0, pre_a, back_a)

    def two(n, carry):
        front(2 * n + 1, pre_b, back_b)
        middle(pre_a, back_a, hid_a, grad_a)
        back(2 * n, hid_a, grad_a)
        front(jnp.minimum(2 * n + 2, tiles - 1), pre_a, back_a)
        middle(pre_b, back_b, hid_b, grad_b)
        back(2 * n + 1, hid_b, grad_b)
        return carry

    lax.fori_loop(0, tiles // 2, two, 0)

    for s in range(2):
        for b in range(share):
            rows_s[pl.ds(s * 4 + b, space, stride=8), :] = acc[b * space:(b + 1) * space, s * 128:(s + 1) * 128]
    send3[...] = rows_s[...].reshape(space, 8, 128).astype(BF)
    exchange(send3, recv3, send_sem.at[2], recv_sem.at[2], me, space)

    def narrow(src, dst):
        def body(n, carry):
            dst[pl.ds(n * 4, 4)] = src[pl.ds(pl.multiple_of(n * 512, 512), 512), :].reshape(4, 128, 128).astype(BF)
            return carry

        lax.fori_loop(0, 8, body, 0)

    narrow(wide, out_p)
    store_p = pltpu.make_async_copy(out_p, pred_hbm, store_sem.at[0])
    store_p.start()
    narrow(part, out_f)
    store_f = pltpu.make_async_copy(out_f, part_hbm, store_sem.at[1])
    store_f.start()
    arrive(send3, recv3, send_sem.at[2], recv_sem.at[2], me, space)

    got = recv3[...].astype(F32).reshape(space * 8, 128).astype(BF)
    full = dot(kron_ref[...], got)
    cgrad = (full[0:128, 0:CH] + full[128:256, CH:128]) * SYN
    team_w[:, CH:128] = cgrad
    back = []
    for k in range(MODES):
        back.append(dot(cgrad[k * 8:k * 8 + 8, :].astype(BF), w_ref[k], ((1,), (1,))))
    back = jnp.where(mask_mode, jnp.concatenate(back, axis=0), 0.0).astype(BF)
    back = jnp.where(mask_field, dot(back, lift_bigt) * ANA, 0.0).astype(BF)
    lanes = iota((space, 128), 1)
    out = jnp.where(lanes % 2 == 0, dot(rep0t_ref[...], back), dot(rep1t_ref[...], back))
    send4[...] = out.reshape(space, 1, 128)
    exchange(send4, recv4, send_sem.at[3], recv_sem.at[3], me, space)

    team[my_dp] = team_w[...].astype(BF)
    copies = []
    for step in range(1, dp):
        copies.append(pltpu.make_async_remote_copy(
            src_ref=team.at[my_dp],
            dst_ref=team.at[my_dp],
            send_sem=send_sem.at[3 + step],
            recv_sem=recv_sem.at[3 + step],
            device_id={"dp": lax.rem(my_dp + step, dp)},
            device_id_type=MESH,
        ))
        copies[-1].start()
    for copy in copies:
        copy.wait()
    team_ref[...] = team[...]
    arrive(send4, recv4, send_sem.at[3], recv_sem.at[3], me, space)
    last_ref[...] = recv4[...].reshape(space, 128)
    store_p.wait()
    store_f.wait()


def finish(
    space, dp, pred_in, part_in, last_ref, team_ref, wavez_ref, pairyt_ref,
    pred_hbm, mode_hbm, field_hbm,
    part, out, mode_out, inner, load_sem, store_sem,
):
    share = MODES * MODES // space
    groups = 4
    each = ROWS // groups
    store_p = pltpu.make_async_copy(pred_in, pred_hbm, store_sem.at[0])
    store_p.start()
    load_p = pltpu.make_async_copy(part_in, part, load_sem)
    load_p.start()

    m_row, m_lane = iota((32, 256), 0), iota((32, 256), 1)
    mask_team = m_row % 4 == m_lane // CH
    for k in range(MODES):
        rows = jnp.concatenate([team_ref[d].astype(F32)[k * 8:k * 8 + 8, :] for d in range(dp)], axis=0)
        left = jnp.where(mask_team, jnp.concatenate([rows[:, 0:CH]] * 4, axis=1), 0.0)
        mode_out[k] = dot(left.T.astype(BF), rows[:, CH:128].astype(BF))
    store_m = pltpu.make_async_copy(mode_out, mode_hbm, store_sem.at[1])
    store_m.start()

    turned = last_ref[...].T
    field = jnp.concatenate([turned[b * 32:(b + 1) * 32] for b in range(share)], axis=1).astype(BF)
    spread = (iota((512, ROWS), 0) // MODES == iota((512, ROWS), 1)).astype(F32).astype(BF)
    s_row, s_lane = iota((512, 256), 0), iota((512, 256), 1)
    value = jnp.where(s_row % MODES == s_lane % space // share, dot(spread, field), 0.0).astype(BF)
    inner[...] = dot(value, wavez_ref[...]).astype(BF)
    load_p.wait()
    stores = []
    for g in range(groups):
        for n in range(g * each // 2, (g + 1) * each // 2):
            value = dot(pairyt_ref[...], inner[n * 32:n * 32 + 32, :]).reshape(2, GRID, GRID)
            out[2 * n:2 * n + 2] = (part[2 * n:2 * n + 2].astype(F32) + value).astype(BF)
        cut = pl.ds(g * each, each)
        stores.append(pltpu.make_async_copy(out.at[cut], field_hbm.at[cut], store_sem.at[2 + g]))
        stores[-1].start()
    store_p.wait()
    store_m.wait()
    for copy in stores:
        copy.wait()


def solution(mesh):
    space, dp = mesh.shape["space"], mesh.shape["dp"]
    consts = tables(space)

    def local(fields, lift_weight, mode_weight, local_weight, project_weight, out_cotangent):
        planes = (ROWS, GRID, GRID)
        hbm = pl.BlockSpec(memory_space=pl.ANY)
        vmem = pl.BlockSpec(memory_space=pltpu.VMEM)
        share = MODES * MODES // space
        small = [jnp.asarray(c) for c in consts[1:]]
        guess, part, last, team = pl.pallas_call(
            functools.partial(kernel, space, dp),
            out_shape=(
                jax.ShapeDtypeStruct(planes, BF),
                jax.ShapeDtypeStruct(planes, BF),
                jax.ShapeDtypeStruct((space, 128), F32),
                jax.ShapeDtypeStruct((dp, 128, 128), BF),
            ),
            in_specs=[hbm] * 4 + [vmem] * 11,
            out_specs=(hbm, hbm, vmem, vmem),
            scratch_shapes=[
                pltpu.VMEM((256, PIX), BF),
                pltpu.VMEM((MODES, share * CH, CH), BF),
                pltpu.VMEM(planes, BF),
                pltpu.VMEM(planes, BF),
                pltpu.VMEM((ROWS * GRID, GRID), F32),
                pltpu.VMEM((ROWS, PIX), BF),
                pltpu.VMEM((ROWS, PIX), BF),
                pltpu.VMEM((ROWS * GRID, GRID), F32),
                pltpu.VMEM(planes, BF),
                pltpu.VMEM(planes, BF),
                pltpu.VMEM((512, 128), BF),
                pltpu.VMEM((256, TILE), F32),
                pltpu.VMEM((256, TILE), F32),
                pltpu.VMEM((256, TILE), BF),
                pltpu.VMEM((256, TILE), BF),
                pltpu.VMEM((256, TILE), F32),
                pltpu.VMEM((256, TILE), F32),
                pltpu.VMEM((256, TILE), BF),
                pltpu.VMEM((256, TILE), BF),
                pltpu.VMEM((256, 256), F32),
                pltpu.VMEM((256, 256), BF),
                pltpu.VMEM((space * 8, 128), F32),
                pltpu.VMEM((128, 256), F32),
                pltpu.VMEM((space, 1, 128), F32),
                pltpu.VMEM((space, 1, 128), F32),
                pltpu.VMEM((space, 8, 128), BF),
                pltpu.VMEM((space, 8, 128), BF),
                pltpu.VMEM((space, 8, 128), BF),
                pltpu.VMEM((space, 8, 128), BF),
                pltpu.VMEM((space, 1, 128), F32),
                pltpu.VMEM((space, 1, 128), F32),
                pltpu.VMEM((dp, 128, 128), BF),
                pltpu.VMEM((128, 128), F32),
                pltpu.SemaphoreType.DMA((11,)),
                pltpu.SemaphoreType.DMA((2,)),
                pltpu.SemaphoreType.DMA((3 + dp,)),
                pltpu.SemaphoreType.DMA((3 + dp,)),
            ],
            compiler_params=pltpu.CompilerParams(
                collective_id=0, has_side_effects=True, vmem_limit_bytes=56 * 1024 * 1024
            ),
        )(
            fields.reshape(planes),
            out_cotangent.reshape(planes),
            mode_weight.reshape(MODES, share * CH, CH),
            jnp.asarray(consts[0]),
            lift_weight,
            local_weight,
            project_weight.T,
            *small[:8],
        )
        prediction, mode_grad, field_grad = pl.pallas_call(
            functools.partial(finish, space, dp),
            out_shape=(
                jax.ShapeDtypeStruct(planes, BF),
                jax.ShapeDtypeStruct((MODES, share * CH, CH), F32),
                jax.ShapeDtypeStruct(planes, BF),
            ),
            in_specs=[hbm] * 2 + [vmem] * 4,
            out_specs=(hbm, hbm, hbm),
            scratch_shapes=[
                pltpu.VMEM(planes, BF),
                pltpu.VMEM(planes, BF),
                pltpu.VMEM((MODES, share * CH, CH), F32),
                pltpu.VMEM((512, 128), BF),
                pltpu.SemaphoreType.DMA,
                pltpu.SemaphoreType.DMA((6,)),
            ],
            compiler_params=pltpu.CompilerParams(vmem_limit_bytes=60 * 1024 * 1024),
        )(guess, part, last, team, small[6], small[8])
        return (
            prediction.reshape(fields.shape),
            mode_grad.reshape(mode_weight.shape),
            field_grad.reshape(fields.shape),
        )

    wide = P("dp", None, "space", None, None)
    return jax.shard_map(
        local,
        mesh=mesh,
        in_specs=(wide, P(), P(None, "space", None, None), P(), P(), wide),
        out_specs=(wide, P(None, "space", None, None), wide),
        check_vma=False,
    )
```

```python
import functools
import math

import jax
import jax.numpy as jnp
import ml_dtypes
import numpy as np
from jax import lax
from jax.experimental import pallas as pl
from jax.experimental.pallas import tpu as pltpu
from jax.sharding import PartitionSpec as P

F32 = jnp.float32
BF = jnp.bfloat16
MESH = pl.DeviceIdType.MESH

GRID = 128
FIELDS = 8
CH = 64
MODES = 16
PIX = GRID * GRID
ROWS = 32
TILE = 1024
ANA = 1.0 / 512.0
SYN = 8.0 ** -1.5


def dot(a, b, dims=((1,), (0,))):
    return lax.dot_general(a, b, (dims, ((), ())), preferred_element_type=F32)


def waves():
    order = np.arange(MODES)
    angle = 2.0 * np.pi * ((order[:, None] + 1) // 2 * np.arange(GRID)[None, :] % GRID) / GRID
    return np.where((order % 2 == 0)[:, None], np.cos(angle), np.sin(angle))


def half(x):
    return np.asarray(x, np.float32).astype(ml_dtypes.bfloat16)


def tables(space):
    w = waves()
    share = MODES * MODES // space
    row = np.arange(MODES * MODES)
    mode = share * (row % space) + row // space
    grid = (w[mode // MODES][:, :, None] * w[mode % MODES][:, None, :]).reshape(MODES * MODES, PIX)
    a0, a1 = w[:, 0::2], w[:, 1::2]
    rep0 = np.repeat(a0, 8, axis=0)
    rep1 = np.repeat(a1, 8, axis=0)
    eye = np.eye(8)
    wave_z = w[mode % MODES]
    pair_y = np.kron(np.eye(2), w)
    kron = np.concatenate([np.kron(a0, eye), np.kron(a1, eye)], axis=0)
    return half(grid), half(rep0), half(rep1), half(rep0.T), half(rep1.T), half(kron), half(kron.T), half(wave_z), half(pair_y), half(pair_y.T)


def iota(shape, axis):
    return lax.broadcasted_iota(jnp.int32, shape, axis)


def activation(v, back):
    normal = 0.5 + 0.5 * lax.erf(v * math.sqrt(0.5))
    e = jnp.exp2((v * v) * (-0.5 / math.log(2.0)))
    grad = back * (normal + v * (e * (1.0 / math.sqrt(2.0 * math.pi))))
    return v * normal, grad


def hops(step):
    x, z, y = step
    return min(x, 4 - x) + min(z, 8 - z) + y


STEPS = sorted(
    [(x, z, y) for x in range(4) for z in range(8) for y in range(2) if x or z or y],
    key=hops, reverse=True,
)


def exchange(src, dst, send_sem, recv_sem, me, space):
    x, z, y = me // 16, me // 2 % 8, me % 2
    for dx, dz, dy in STEPS:
        to = lax.rem(x + dx, 4) * 16 + lax.rem(z + dz, 8) * 2 + lax.rem(y + dy, 2)
        pltpu.make_async_remote_copy(
            src_ref=src.at[to],
            dst_ref=dst.at[me],
            send_sem=send_sem,
            recv_sem=recv_sem,
            device_id={"space": to},
            device_id_type=MESH,
        ).start()
    dst[me] = src[me]


def arrive(src, dst, send_sem, recv_sem, me, space):
    whole = pltpu.make_async_remote_copy(
        src_ref=src.at[pl.ds(0, space - 1)],
        dst_ref=dst.at[pl.ds(0, space - 1)],
        send_sem=send_sem,
        recv_sem=recv_sem,
        device_id={"space": lax.rem(me + 1, space)},
        device_id_type=MESH,
    )
    whole.wait_send()
    whole.wait_recv()


def kernel(
    space, dp,
    f_hbm, c_hbm, w_hbm, t_hbm, lift_ref, local_ref, project_ref,
    rep0_ref, rep1_ref, rep0t_ref, rep1t_ref, kron_ref, kront_ref, wavez_ref, pairy_ref,
    pred_hbm, part_hbm, last_ref, team_ref,
    t_ref, w_ref, raw_f, raw_c, wide, flat_f, flat_c, part, out_p, out_f, part_y,
    pre_a, grad_a, pre_b, grad_b, hid, bg, acc, planes, rows_s, stack,
    send1, recv1, send2, recv2, send3, recv3, send4, recv4, team, team_w,
    load_sem, store_sem, send_sem, recv_sem,
):
    me = lax.axis_index("space")
    my_dp = lax.axis_index("dp")
    share = MODES * MODES // space
    chunks = 8
    width = PIX // chunks

    load_f = pltpu.make_async_copy(f_hbm, raw_f, load_sem.at[0])
    load_f.start()
    load_t = []
    for n in range(chunks):
        cut = pl.ds(n * width, width)
        load_t.append(pltpu.make_async_copy(t_hbm.at[:, cut], t_ref.at[:, cut], load_sem.at[3 + n]))
        load_t[-1].start()
    load_c = pltpu.make_async_copy(c_hbm, raw_c, load_sem.at[1])
    load_c.start()
    load_w = pltpu.make_async_copy(w_hbm, w_ref, load_sem.at[2])
    load_w.start()

    barrier = pltpu.get_barrier_semaphore()

    def greet(step, carry):
        pl.semaphore_signal(barrier, inc=1, device_id={"space": lax.rem(me + step, space)}, device_id_type=MESH)
        return carry

    lax.fori_loop(1, space, greet, 0)
    for step in range(1, dp):
        pl.semaphore_signal(barrier, inc=1, device_id={"dp": lax.rem(my_dp + step, dp)}, device_id_type=MESH)

    lift = lift_ref[...]
    pick32 = (iota((ROWS, FIELDS), 0) // 2 % FIELDS == iota((ROWS, FIELDS), 1)).astype(F32).astype(BF)
    pick128 = (iota((128, FIELDS), 0) // 2 % FIELDS == iota((128, FIELDS), 1)).astype(F32).astype(BF)
    p_row, q_lane = iota((ROWS, 256), 0), iota((ROWS, 256), 1)
    same = (p_row // 16 == q_lane // 128) & (p_row % 2 == q_lane // CH % 2)
    both = dot(lift, local_ref[...]).astype(BF)
    both32 = dot(pick32, both)
    both32 = jnp.where(same, jnp.concatenate([both32] * 4, axis=1), 0.0)
    proj32 = dot(pick32, project_ref[...])
    proj32 = jnp.where(same, jnp.concatenate([proj32] * 4, axis=1), 0.0)
    down_field = both32.astype(BF)
    down_proj = proj32.astype(BF)
    up_field = both32.T.astype(BF)
    up_proj = proj32.T.astype(BF)
    lift128 = dot(pick128, lift)
    lift_big = jnp.concatenate([lift128] * 4, axis=1)
    lift_bigt = lift_big.T.astype(BF)
    lift_big = lift_big.astype(BF)
    r128, l128 = iota((128, 128), 0), iota((128, 128), 1)
    mask_field = (r128 % 4 == l128 // 32) & (r128 // 4 % 2 == l128 // 16 % 2)
    first_plane = l128 % 2 == 0
    r256, l256 = iota((128, 256), 0), iota((128, 256), 1)
    mask_mode = r256 % 4 == l256 // CH

    def relayout(raw, flat):
        def widen(n, carry):
            cut = pl.ds(n * 4, 4)
            wide[pl.ds(pl.multiple_of(n * 512, 512), 512), :] = raw[cut].astype(F32).reshape(512, 128)
            return carry

        lax.fori_loop(0, 8, widen, 0)

        def turn(n, carry):
            for u in range(8):
                y = n * 8 + u
                rows = wide[pl.ds(y, ROWS, stride=GRID), :]
                flat[:, pl.ds(pl.multiple_of(y * GRID, GRID), GRID)] = rows.astype(BF)
            return carry

        lax.fori_loop(0, GRID // 8, turn, 0)

    load_f.wait()
    for n in range(ROWS // 2):
        pair = raw_f[2 * n:2 * n + 2].reshape(2 * GRID, GRID)
        part_y[n * 32:n * 32 + 32, :] = dot(pairy_ref[...], pair).astype(BF)
    value = dot(part_y[...], wavez_ref[...], ((1,), (1,)))
    s_row, s_lane = iota((512, 256), 0), iota((512, 256), 1)
    value = jnp.where(s_row % MODES == s_lane % space // share, value, 0.0).astype(BF)
    fold = (iota((ROWS, 512), 0) == iota((ROWS, 512), 1) // MODES).astype(F32).astype(BF)
    spec = dot(fold, value).T
    send1[...] = jnp.concatenate([spec[b * space:(b + 1) * space] for b in range(share)], axis=1).reshape(space, 1, 128)

    pl.semaphore_wait(barrier, space - 1 + dp - 1)
    exchange(send1, recv1, send_sem.at[0], recv_sem.at[0], me, space)
    relayout(raw_f, flat_f)
    load_c.wait()
    relayout(raw_c, flat_c)
    load_w.wait()
    arrive(send1, recv1, send_sem.at[0], recv_sem.at[0], me, space)

    got = recv1[...].reshape(space, 128).astype(BF)
    coef = jnp.where(first_plane, dot(rep0_ref[...], got), dot(rep1_ref[...], got)) * ANA
    coef = jnp.where(mask_field, coef, 0.0).astype(BF)
    coef = dot(coef, lift_big)
    team_w[:, 0:CH] = coef[:, 0:CH]
    stack[...] = jnp.where(mask_mode, coef, 0.0)
    mixed = []
    for k in range(MODES):
        mixed.append(dot(stack[k * 8:k * 8 + 8, :].astype(BF), w_ref[k]))
    mixed = (jnp.concatenate(mixed, axis=0) * SYN).astype(BF)
    out = jnp.concatenate(
        [dot(kront_ref[:, 0:128], mixed), dot(kront_ref[:, 128:256], mixed)], axis=1
    )
    send2[...] = out.reshape(space, 8, 128).astype(BF)
    exchange(send2, recv2, send_sem.at[1], recv_sem.at[1], me, space)
    acc[...] = jnp.zeros_like(acc)
    tiles = PIX // TILE

    def up(n, carry):
        cut = pl.ds(pl.multiple_of(n * TILE, TILE), TILE)
        bg[n] = dot(up_proj, flat_c[:, cut]).astype(BF)
        return carry

    lax.fori_loop(0, tiles, up, 0)
    for copy in load_t:
        copy.wait()
    arrive(send2, recv2, send_sem.at[1], recv_sem.at[1], me, space)

    rows_s[...] = recv2[...].astype(F32).reshape(space * 8, 128)
    for s in range(2):
        for b in range(share):
            block = rows_s[pl.ds(s * 4 + b, space, stride=8), :]
            planes[s * 128:(s + 1) * 128, b * space:(b + 1) * space] = block.T.astype(BF)

    def columns(n):
        return pl.ds(pl.multiple_of(n * TILE, TILE), TILE)

    def front(n, pre_s):
        pre_s[...] = dot(planes[...], t_ref[:, columns(n)]) + dot(up_field, flat_f[:, columns(n)])

    def middle(n, pre_s, grad_s):
        for r in range(0, 256, 32):
            for c in range(0, TILE, 512):
                at = (slice(r, r + 32), slice(c, c + 512))
                hidden, grad = activation(pre_s[at], bg[(n,) + at].astype(F32))
                hid[(n,) + at] = hidden.astype(BF)
                grad = grad.astype(BF)
                bg[(n,) + at] = grad
                grad_s[at] = grad

    def back(n, grad_s):
        acc[...] += dot(t_ref[:, columns(n)], grad_s[...], ((1,), (1,)))

    front(0, pre_a)

    def two(n, carry):
        front(2 * n + 1, pre_b)
        middle(2 * n, pre_a, grad_a)
        back(2 * n, grad_a)
        front(jnp.minimum(2 * n + 2, tiles - 1), pre_a)
        middle(2 * n + 1, pre_b, grad_b)
        back(2 * n + 1, grad_b)
        return carry

    lax.fori_loop(0, tiles // 2, two, 0)

    for s in range(2):
        for b in range(share):
            rows_s[pl.ds(s * 4 + b, space, stride=8), :] = acc[b * space:(b + 1) * space, s * 128:(s + 1) * 128]
    send3[...] = rows_s[...].reshape(space, 8, 128).astype(BF)
    exchange(send3, recv3, send_sem.at[2], recv_sem.at[2], me, space)

    def narrow(src, dst):
        def body(n, carry):
            dst[pl.ds(n * 4, 4)] = src[pl.ds(pl.multiple_of(n * 512, 512), 512), :].reshape(4, 128, 128).astype(BF)
            return carry

        lax.fori_loop(0, 8, body, 0)

    def down(n, carry):
        guess = dot(down_proj, hid[n])
        local = dot(down_field, bg[n])
        for u in range(TILE // GRID):
            y = n * (TILE // GRID) + u
            wide[pl.ds(y, ROWS, stride=GRID), :] = guess[:, u * GRID:(u + 1) * GRID]
            part[pl.ds(y, ROWS, stride=GRID), :] = local[:, u * GRID:(u + 1) * GRID]
        return carry

    lax.fori_loop(0, tiles, down, 0)
    narrow(wide, out_p)
    store_p = pltpu.make_async_copy(out_p, pred_hbm, store_sem.at[0])
    store_p.start()
    narrow(part, out_f)
    store_f = pltpu.make_async_copy(out_f, part_hbm, store_sem.at[1])
    store_f.start()
    arrive(send3, recv3, send_sem.at[2], recv_sem.at[2], me, space)

    got = recv3[...].astype(F32).reshape(space * 8, 128).astype(BF)
    full = dot(kron_ref[...], got)
    cgrad = (full[0:128, 0:CH] + full[128:256, CH:128]) * SYN
    team_w[:, CH:128] = cgrad
    back = []
    for k in range(MODES):
        back.append(dot(cgrad[k * 8:k * 8 + 8, :].astype(BF), w_ref[k], ((1,), (1,))))
    back = jnp.where(mask_mode, jnp.concatenate(back, axis=0), 0.0).astype(BF)
    back = jnp.where(mask_field, dot(back, lift_bigt) * ANA, 0.0).astype(BF)
    lanes = iota((space, 128), 1)
    out = jnp.where(lanes % 2 == 0, dot(rep0t_ref[...], back), dot(rep1t_ref[...], back))
    send4[...] = out.reshape(space, 1, 128)
    exchange(send4, recv4, send_sem.at[3], recv_sem.at[3], me, space)

    team[my_dp] = team_w[...].astype(BF)
    copies = []
    for step in range(1, dp):
        copies.append(pltpu.make_async_remote_copy(
            src_ref=team.at[my_dp],
            dst_ref=team.at[my_dp],
            send_sem=send_sem.at[3 + step],
            recv_sem=recv_sem.at[3 + step],
            device_id={"dp": lax.rem(my_dp + step, dp)},
            device_id_type=MESH,
        ))
        copies[-1].start()
    for copy in copies:
        copy.wait()
    team_ref[...] = team[...]
    arrive(send4, recv4, send_sem.at[3], recv_sem.at[3], me, space)
    last_ref[...] = recv4[...].reshape(space, 128)
    store_p.wait()
    store_f.wait()


def finish(
    space, dp, pred_in, part_in, last_ref, team_ref, wavez_ref, pairyt_ref,
    pred_hbm, mode_hbm, field_hbm,
    pred, part, out, mode_out, inner, load_sem, store_sem,
):
    share = MODES * MODES // space
    groups = 4
    each = ROWS // groups
    load_q = pltpu.make_async_copy(pred_in, pred, load_sem.at[1])
    load_q.start()
    load_p = pltpu.make_async_copy(part_in, part, load_sem.at[0])
    load_p.start()

    load_q.wait()
    store_p = pltpu.make_async_copy(pred, pred_hbm, store_sem.at[0])
    store_p.start()
    m_row, m_lane = iota((32, 256), 0), iota((32, 256), 1)
    mask_team = m_row % 4 == m_lane // CH
    for k in range(MODES):
        rows = jnp.concatenate([team_ref[d].astype(F32)[k * 8:k * 8 + 8, :] for d in range(dp)], axis=0)
        left = jnp.where(mask_team, jnp.concatenate([rows[:, 0:CH]] * 4, axis=1), 0.0)
        mode_out[k] = dot(left.T.astype(BF), rows[:, CH:128].astype(BF))
    store_m = pltpu.make_async_copy(mode_out, mode_hbm, store_sem.at[1])
    store_m.start()

    turned = last_ref[...].T
    field = jnp.concatenate([turned[b * 32:(b + 1) * 32] for b in range(share)], axis=1).astype(BF)
    spread = (iota((512, ROWS), 0) // MODES == iota((512, ROWS), 1)).astype(F32).astype(BF)
    s_row, s_lane = iota((512, 256), 0), iota((512, 256), 1)
    value = jnp.where(s_row % MODES == s_lane % space // share, dot(spread, field), 0.0).astype(BF)
    inner[...] = dot(value, wavez_ref[...]).astype(BF)
    load_p.wait()
    stores = []
    for g in range(groups):
        for n in range(g * each // 2, (g + 1) * each // 2):
            value = dot(pairyt_ref[...], inner[n * 32:n * 32 + 32, :]).reshape(2, GRID, GRID)
            out[2 * n:2 * n + 2] = (part[2 * n:2 * n + 2].astype(F32) + value).astype(BF)
        cut = pl.ds(g * each, each)
        stores.append(pltpu.make_async_copy(out.at[cut], field_hbm.at[cut], store_sem.at[2 + g]))
        stores[-1].start()
    store_p.wait()
    store_m.wait()
    for copy in stores:
        copy.wait()


def solution(mesh):
    space, dp = mesh.shape["space"], mesh.shape["dp"]
    consts = tables(space)

    def local(fields, lift_weight, mode_weight, local_weight, project_weight, out_cotangent):
        planes = (ROWS, GRID, GRID)
        hbm = pl.BlockSpec(memory_space=pl.ANY)
        vmem = pl.BlockSpec(memory_space=pltpu.VMEM)
        share = MODES * MODES // space
        small = [jnp.asarray(c) for c in consts[1:]]
        guess, part, last, team = pl.pallas_call(
            functools.partial(kernel, space, dp),
            out_shape=(
                jax.ShapeDtypeStruct(planes, BF),
                jax.ShapeDtypeStruct(planes, BF),
                jax.ShapeDtypeStruct((space, 128), F32),
                jax.ShapeDtypeStruct((dp, 128, 128), BF),
            ),
            in_specs=[hbm] * 4 + [vmem] * 11,
            out_specs=(hbm, hbm, vmem, vmem),
            scratch_shapes=[
                pltpu.VMEM((256, PIX), BF),
                pltpu.VMEM((MODES, share * CH, CH), BF),
                pltpu.VMEM(planes, BF),
                pltpu.VMEM(planes, BF),
                pltpu.VMEM((ROWS * GRID, GRID), F32),
                pltpu.VMEM((ROWS, PIX), BF),
                pltpu.VMEM((ROWS, PIX), BF),
                pltpu.VMEM((ROWS * GRID, GRID), F32),
                pltpu.VMEM(planes, BF),
                pltpu.VMEM(planes, BF),
                pltpu.VMEM((512, 128), BF),
                pltpu.VMEM((256, TILE), F32),
                pltpu.VMEM((256, TILE), BF),
                pltpu.VMEM((256, TILE), F32),
                pltpu.VMEM((256, TILE), BF),
                pltpu.VMEM((PIX // TILE, 256, TILE), BF),
                pltpu.VMEM((PIX // TILE, 256, TILE), BF),
                pltpu.VMEM((256, 256), F32),
                pltpu.VMEM((256, 256), BF),
                pltpu.VMEM((space * 8, 128), F32),
                pltpu.VMEM((128, 256), F32),
                pltpu.VMEM((space, 1, 128), F32),
                pltpu.VMEM((space, 1, 128), F32),
                pltpu.VMEM((space, 8, 128), BF),
                pltpu.VMEM((space, 8, 128), BF),
                pltpu.VMEM((space, 8, 128), BF),
                pltpu.VMEM((space, 8, 128), BF),
                pltpu.VMEM((space, 1, 128), F32),
                pltpu.VMEM((space, 1, 128), F32),
                pltpu.VMEM((dp, 128, 128), BF),
                pltpu.VMEM((128, 128), F32),
                pltpu.SemaphoreType.DMA((11,)),
                pltpu.SemaphoreType.DMA((2,)),
                pltpu.SemaphoreType.DMA((3 + dp,)),
                pltpu.SemaphoreType.DMA((3 + dp,)),
            ],
            compiler_params=pltpu.CompilerParams(
                collective_id=0, has_side_effects=True, vmem_limit_bytes=56 * 1024 * 1024
            ),
        )(
            fields.reshape(planes),
            out_cotangent.reshape(planes),
            mode_weight.reshape(MODES, share * CH, CH),
            jnp.asarray(consts[0]),
            lift_weight,
            local_weight,
            project_weight.T,
            *small[:8],
        )
        prediction, mode_grad, field_grad = pl.pallas_call(
            functools.partial(finish, space, dp),
            out_shape=(
                jax.ShapeDtypeStruct(planes, BF),
                jax.ShapeDtypeStruct((MODES, share * CH, CH), F32),
                jax.ShapeDtypeStruct(planes, BF),
            ),
            in_specs=[hbm] * 2 + [vmem] * 4,
            out_specs=(hbm, hbm, hbm),
            scratch_shapes=[
                pltpu.VMEM(planes, BF),
                pltpu.VMEM(planes, BF),
                pltpu.VMEM(planes, BF),
                pltpu.VMEM((MODES, share * CH, CH), F32),
                pltpu.VMEM((512, 128), BF),
                pltpu.SemaphoreType.DMA((2,)),
                pltpu.SemaphoreType.DMA((6,)),
            ],
            compiler_params=pltpu.CompilerParams(vmem_limit_bytes=60 * 1024 * 1024),
        )(guess, part, last, team, small[6], small[8])
        return (
            prediction.reshape(fields.shape),
            mode_grad.reshape(mode_weight.shape),
            field_grad.reshape(fields.shape),
        )

    wide = P("dp", None, "space", None, None)
    return jax.shard_map(
        local,
        mesh=mesh,
        in_specs=(wide, P(), P(None, "space", None, None), P(), P(), wide),
        out_specs=(wide, P(None, "space", None, None), wide),
        check_vma=False,
    )
```

```python
import functools
import math

import jax
import jax.numpy as jnp
import ml_dtypes
import numpy as np
from jax import lax
from jax.experimental import pallas as pl
from jax.experimental.pallas import tpu as pltpu
from jax.sharding import PartitionSpec as P

F32 = jnp.float32
BF = jnp.bfloat16
MESH = pl.DeviceIdType.MESH

GRID = 128
FIELDS = 8
CH = 64
MODES = 16
PIX = GRID * GRID
ROWS = 32
TILE = 1024
ANA = 1.0 / 512.0
SYN = 8.0 ** -1.5
ROOT = math.sqrt(0.5)


def dot(a, b, dims=((1,), (0,))):
    return lax.dot_general(a, b, (dims, ((), ())), preferred_element_type=F32)


def waves():
    order = np.arange(MODES)
    angle = 2.0 * np.pi * ((order[:, None] + 1) // 2 * np.arange(GRID)[None, :] % GRID) / GRID
    return np.where((order % 2 == 0)[:, None], np.cos(angle), np.sin(angle))


def half(x):
    return np.asarray(x, np.float32).astype(ml_dtypes.bfloat16)


def tables(space):
    w = waves()
    share = MODES * MODES // space
    row = np.arange(MODES * MODES)
    mode = share * (row % space) + row // space
    grid = (w[mode // MODES][:, :, None] * w[mode % MODES][:, None, :]).reshape(MODES * MODES, PIX)
    a0, a1 = w[:, 0::2], w[:, 1::2]
    rep0 = np.repeat(a0, 8, axis=0)
    rep1 = np.repeat(a1, 8, axis=0)
    eye = np.eye(8)
    wave_z = w[mode % MODES]
    pair_y = np.kron(np.eye(2), w)
    kron = np.concatenate([np.kron(a0, eye), np.kron(a1, eye)], axis=0)
    return half(grid), half(rep0), half(rep1), half(rep0.T), half(rep1.T), half(kron), half(kron.T), half(wave_z), half(pair_y), half(pair_y.T)


def iota(shape, axis):
    return lax.broadcasted_iota(jnp.int32, shape, axis)


def activation(w, back):
    twice = 1.0 + lax.erf(w)
    e = jnp.exp2((w * w) * (-1.0 / math.log(2.0)))
    slope = twice + w * (e * (2.0 / math.sqrt(math.pi)))
    return (w * twice).astype(BF), slope.astype(BF) * back


def hops(step):
    x, z, y = step
    return min(x, 4 - x) + min(z, 8 - z) + y


STEPS = sorted(
    [(x, z, y) for x in range(4) for z in range(8) for y in range(2) if x or z or y],
    key=hops, reverse=True,
)


def peers(me):
    x, z, y = me // 16, me // 2 % 8, me % 2
    return [lax.rem(x + dx, 4) * 16 + lax.rem(z + dz, 8) * 2 + lax.rem(y + dy, 2) for dx, dz, dy in STEPS]


def exchange(src, dst, send_sem, recv_sem, me, space):
    for to in peers(me):
        pltpu.make_async_remote_copy(
            src_ref=src.at[to],
            dst_ref=dst.at[me],
            send_sem=send_sem,
            recv_sem=recv_sem,
            device_id={"space": to},
            device_id_type=MESH,
        ).start()
    dst[me] = src[me]


def arrive(src, dst, send_sem, recv_sem, me, space):
    whole = pltpu.make_async_remote_copy(
        src_ref=src.at[pl.ds(0, space - 1)],
        dst_ref=dst.at[pl.ds(0, space - 1)],
        send_sem=send_sem,
        recv_sem=recv_sem,
        device_id={"space": lax.rem(me + 1, space)},
        device_id_type=MESH,
    )
    whole.wait_send()
    whole.wait_recv()


def kernel(
    space, dp,
    f_hbm, c_hbm, w_hbm, t_hbm, lift_hbm, local_hbm, project_hbm,
    rep0_hbm, rep1_hbm, rep0t_hbm, rep1t_hbm, kron_hbm, kront_hbm, wavez_hbm, pairy_hbm,
    pred_ref, part_ref, last_ref, team_ref,
    t_ref, w_ref, raw_f, raw_c, wide, flat_f, flat_c, part, part_y,
    pre_a, grad_a, pre_b, grad_b, hid, bg, acc, planes, rows_s, stack,
    send1, recv1, send2, recv2, send3, recv3, send4, recv4, team, team_w,
    lift_ref, local_ref, project_ref, rep0_ref, rep1_ref, rep0t_ref, rep1t_ref, kron_ref, kront_ref, wavez_ref, pairy_ref,
    load_sem, send_sem, recv_sem,
):
    me = lax.axis_index("space")
    my_dp = lax.axis_index("dp")
    share = MODES * MODES // space
    chunks = 8
    width = PIX // chunks

    load_f = pltpu.make_async_copy(f_hbm, raw_f, load_sem.at[0])
    load_f.start()
    load_z = pltpu.make_async_copy(wavez_hbm, wavez_ref, load_sem.at[3 + chunks])
    load_z.start()
    load_y = pltpu.make_async_copy(pairy_hbm, pairy_ref, load_sem.at[4 + chunks])
    load_y.start()
    load_s = []
    for n, (src, dst) in enumerate([
        (lift_hbm, lift_ref), (local_hbm, local_ref), (project_hbm, project_ref),
        (rep0_hbm, rep0_ref), (rep1_hbm, rep1_ref), (rep0t_hbm, rep0t_ref), (rep1t_hbm, rep1t_ref),
        (kron_hbm, kron_ref), (kront_hbm, kront_ref),
    ]):
        load_s.append(pltpu.make_async_copy(src, dst, load_sem.at[5 + chunks + n]))
        load_s[-1].start()
    load_t = []
    for n in range(chunks):
        cut = pl.ds(n * width, width)
        load_t.append(pltpu.make_async_copy(t_hbm.at[:, cut], t_ref.at[:, cut], load_sem.at[3 + n]))
        load_t[-1].start()
    load_c = pltpu.make_async_copy(c_hbm, raw_c, load_sem.at[1])
    load_c.start()
    load_w = pltpu.make_async_copy(w_hbm, w_ref, load_sem.at[2])
    load_w.start()

    barrier = pltpu.get_barrier_semaphore()

    for to in peers(me):
        pl.semaphore_signal(barrier, inc=1, device_id={"space": to}, device_id_type=MESH)
    for step in range(1, dp):
        pl.semaphore_signal(barrier, inc=1, device_id={"dp": lax.rem(my_dp + step, dp)}, device_id_type=MESH)

    def relayout(raw, flat):
        def widen(n, carry):
            cut = pl.ds(n * 4, 4)
            wide[pl.ds(pl.multiple_of(n * 512, 512), 512), :] = raw[cut].astype(F32).reshape(512, 128)
            return carry

        lax.fori_loop(0, 8, widen, 0)

        def turn(n, carry):
            for u in range(8):
                y = n * 8 + u
                rows = wide[pl.ds(y, ROWS, stride=GRID), :]
                flat[:, pl.ds(pl.multiple_of(y * GRID, GRID), GRID)] = rows.astype(BF)
            return carry

        lax.fori_loop(0, GRID // 8, turn, 0)

    load_f.wait()
    load_z.wait()
    load_y.wait()
    for n in range(ROWS // 2):
        pair = raw_f[2 * n:2 * n + 2].reshape(2 * GRID, GRID)
        part_y[n * 32:n * 32 + 32, :] = dot(pairy_ref[...], pair).astype(BF)
    value = dot(part_y[...], wavez_ref[...], ((1,), (1,)))
    s_row, s_lane = iota((512, 256), 0), iota((512, 256), 1)
    value = jnp.where(s_row % MODES == s_lane % space // share, value, 0.0).astype(BF)
    fold = (iota((ROWS, 512), 0) == iota((ROWS, 512), 1) // MODES).astype(F32).astype(BF)
    spec = dot(fold, value).T
    send1[...] = jnp.concatenate([spec[b * space:(b + 1) * space] for b in range(share)], axis=1).reshape(space, 1, 128)

    pl.semaphore_wait(barrier, space - 1 + dp - 1)
    exchange(send1, recv1, send_sem.at[0], recv_sem.at[0], me, space)
    for copy in load_s:
        copy.wait()
    lift = lift_ref[...]
    pick32 = (iota((ROWS, FIELDS), 0) // 2 % FIELDS == iota((ROWS, FIELDS), 1)).astype(F32).astype(BF)
    pick128 = (iota((128, FIELDS), 0) // 2 % FIELDS == iota((128, FIELDS), 1)).astype(F32).astype(BF)
    p_row, q_lane = iota((ROWS, 256), 0), iota((ROWS, 256), 1)
    same = (p_row // 16 == q_lane // 128) & (p_row % 2 == q_lane // CH % 2)
    both = dot(lift, local_ref[...])
    both = jnp.concatenate([both[n // 2 % FIELDS:n // 2 % FIELDS + 1] for n in range(ROWS)], axis=0)
    both32 = jnp.where(same, jnp.concatenate([both] * 4, axis=1), 0.0)
    proj32 = dot(pick32, project_ref[...])
    proj32 = jnp.where(same, jnp.concatenate([proj32] * 4, axis=1), 0.0)
    down_field = both32.astype(BF)
    down_proj = proj32.astype(BF)
    up_field = (both32 * ROOT).T.astype(BF)
    up_proj = (proj32 * 0.5).T.astype(BF)
    lift128 = dot(pick128, lift)
    lift_big = jnp.concatenate([lift128] * 4, axis=1)
    lift_bigt = lift_big.T.astype(BF)
    lift_big = lift_big.astype(BF)
    r128, l128 = iota((128, 128), 0), iota((128, 128), 1)
    mask_field = (r128 % 4 == l128 // 32) & (r128 // 4 % 2 == l128 // 16 % 2)
    first_plane = l128 % 2 == 0
    r256, l256 = iota((128, 256), 0), iota((128, 256), 1)
    mask_mode = r256 % 4 == l256 // CH

    relayout(raw_f, flat_f)
    load_c.wait()
    relayout(raw_c, flat_c)
    load_w.wait()
    arrive(send1, recv1, send_sem.at[0], recv_sem.at[0], me, space)

    got = recv1[...].reshape(space, 128).astype(BF)
    coef = jnp.where(first_plane, dot(rep0_ref[...], got), dot(rep1_ref[...], got)) * ANA
    coef = jnp.where(mask_field, coef, 0.0).astype(BF)
    coef = dot(coef, lift_big)
    team_w[:, 0:CH] = coef[:, 0:CH]
    stack[...] = jnp.where(mask_mode, coef, 0.0)
    mixed = []
    for k in range(MODES):
        mixed.append(dot(stack[k * 8:k * 8 + 8, :].astype(BF), w_ref[k]))
    mixed = (jnp.concatenate(mixed, axis=0) * (SYN * ROOT)).astype(BF)
    out = jnp.concatenate(
        [dot(kront_ref[:, 0:128], mixed), dot(kront_ref[:, 128:256], mixed)], axis=1
    )
    send2[...] = out.reshape(space, 8, 128).astype(BF)
    exchange(send2, recv2, send_sem.at[1], recv_sem.at[1], me, space)
    acc[...] = jnp.zeros_like(acc)
    tiles = PIX // TILE

    def up(n, carry):
        cut = pl.ds(pl.multiple_of(n * TILE, TILE), TILE)
        bg[n] = dot(up_proj, flat_c[:, cut]).astype(BF)
        return carry

    lax.fori_loop(0, tiles, up, 0)
    for copy in load_t:
        copy.wait()
    arrive(send2, recv2, send_sem.at[1], recv_sem.at[1], me, space)

    rows_s[...] = recv2[...].astype(F32).reshape(space * 8, 128)
    for s in range(2):
        for b in range(share):
            block = rows_s[pl.ds(s * 4 + b, space, stride=8), :]
            planes[s * 128:(s + 1) * 128, b * space:(b + 1) * space] = block.T.astype(BF)

    def columns(n):
        return pl.ds(pl.multiple_of(n * TILE, TILE), TILE)

    def front(n, pre_s):
        pre_s[...] = dot(planes[...], t_ref[:, columns(n)]) + dot(up_field, flat_f[:, columns(n)])

    def middle(n, pre_s, grad_s):
        for r in range(0, 256, 32):
            for c in range(0, TILE, 512):
                at = (slice(r, r + 32), slice(c, c + 512))
                hidden, grad = activation(pre_s[at], bg[(n,) + at])
                hid[(n,) + at] = hidden
                bg[(n,) + at] = grad
                grad_s[at] = grad

    def back(n, grad_s):
        acc[...] += dot(t_ref[:, columns(n)], grad_s[...], ((1,), (1,)))

    front(0, pre_a)

    def two(n, carry):
        front(2 * n + 1, pre_b)
        middle(2 * n, pre_a, grad_a)
        back(2 * n, grad_a)
        front(jnp.minimum(2 * n + 2, tiles - 1), pre_a)
        middle(2 * n + 1, pre_b, grad_b)
        back(2 * n + 1, grad_b)
        return carry

    lax.fori_loop(0, tiles // 2, two, 0)

    for s in range(2):
        for b in range(share):
            rows_s[pl.ds(s * 4 + b, space, stride=8), :] = acc[b * space:(b + 1) * space, s * 128:(s + 1) * 128]
    send3[...] = rows_s[...].reshape(space, 8, 128).astype(BF)
    exchange(send3, recv3, send_sem.at[2], recv_sem.at[2], me, space)

    def narrow(src, dst):
        def body(n, carry):
            dst[pl.ds(n * 4, 4)] = src[pl.ds(pl.multiple_of(n * 512, 512), 512), :].reshape(4, 128, 128).astype(BF)
            return carry

        lax.fori_loop(0, 8, body, 0)

    def down(n, carry):
        guess = dot(down_proj, hid[n]) * ROOT
        local = dot(down_field, bg[n])
        for u in range(TILE // GRID):
            y = n * (TILE // GRID) + u
            wide[pl.ds(y, ROWS, stride=GRID), :] = guess[:, u * GRID:(u + 1) * GRID]
            part[pl.ds(y, ROWS, stride=GRID), :] = local[:, u * GRID:(u + 1) * GRID]
        return carry

    lax.fori_loop(0, tiles, down, 0)
    arrive(send3, recv3, send_sem.at[2], recv_sem.at[2], me, space)

    got = recv3[...].astype(F32).reshape(space * 8, 128).astype(BF)
    full = dot(kron_ref[...], got)
    cgrad = (full[0:128, 0:CH] + full[128:256, CH:128]) * SYN
    team_w[:, CH:128] = cgrad
    back = []
    for k in range(MODES):
        back.append(dot(cgrad[k * 8:k * 8 + 8, :].astype(BF), w_ref[k], ((1,), (1,))))
    back = jnp.where(mask_mode, jnp.concatenate(back, axis=0), 0.0).astype(BF)
    back = jnp.where(mask_field, dot(back, lift_bigt) * ANA, 0.0).astype(BF)
    lanes = iota((space, 128), 1)
    out = jnp.where(lanes % 2 == 0, dot(rep0t_ref[...], back), dot(rep1t_ref[...], back))
    send4[...] = out.reshape(space, 1, 128)
    exchange(send4, recv4, send_sem.at[3], recv_sem.at[3], me, space)

    team[my_dp] = team_w[...].astype(BF)
    copies = []
    for step in range(1, dp):
        copies.append(pltpu.make_async_remote_copy(
            src_ref=team.at[my_dp],
            dst_ref=team.at[my_dp],
            send_sem=send_sem.at[3 + step],
            recv_sem=recv_sem.at[3 + step],
            device_id={"dp": lax.rem(my_dp + step, dp)},
            device_id_type=MESH,
        ))
        copies[-1].start()
    narrow(wide, pred_ref)
    narrow(part, part_ref)
    for copy in copies:
        copy.wait()
    team_ref[...] = team[...]
    arrive(send4, recv4, send_sem.at[3], recv_sem.at[3], me, space)
    last_ref[...] = recv4[...].reshape(space, 128)


def finish(
    space, dp, pred, part, last_ref, team_ref, wavez_ref, pairyt_ref,
    pred_hbm, mode_hbm, field_hbm,
    out, mode_out, inner, store_sem,
):
    share = MODES * MODES // space
    groups = 4
    each = ROWS // groups
    store_p = pltpu.make_async_copy(pred, pred_hbm, store_sem.at[0])
    store_p.start()

    m_row, m_lane = iota((32, 256), 0), iota((32, 256), 1)
    mask_team = m_row % 4 == m_lane // CH
    for k in range(MODES):
        rows = jnp.concatenate([team_ref[d].astype(F32)[k * 8:k * 8 + 8, :] for d in range(dp)], axis=0)
        left = jnp.where(mask_team, jnp.concatenate([rows[:, 0:CH]] * 4, axis=1), 0.0)
        mode_out[k] = dot(left.T.astype(BF), rows[:, CH:128].astype(BF))
    store_m = pltpu.make_async_copy(mode_out, mode_hbm, store_sem.at[1])
    store_m.start()

    turned = last_ref[...].T
    field = jnp.concatenate([turned[b * 32:(b + 1) * 32] for b in range(share)], axis=1).astype(BF)
    spread = (iota((512, ROWS), 0) // MODES == iota((512, ROWS), 1)).astype(F32).astype(BF)
    s_row, s_lane = iota((512, 256), 0), iota((512, 256), 1)
    value = jnp.where(s_row % MODES == s_lane % space // share, dot(spread, field), 0.0).astype(BF)
    inner[...] = dot(value, wavez_ref[...]).astype(BF)
    stores = []
    for g in range(groups):
        for n in range(g * each // 2, (g + 1) * each // 2):
            value = dot(pairyt_ref[...], inner[n * 32:n * 32 + 32, :]).reshape(2, GRID, GRID)
            out[2 * n:2 * n + 2] = (part[2 * n:2 * n + 2].astype(F32) + value).astype(BF)
        cut = pl.ds(g * each, each)
        stores.append(pltpu.make_async_copy(out.at[cut], field_hbm.at[cut], store_sem.at[2 + g]))
        stores[-1].start()
    store_p.wait()
    store_m.wait()
    for copy in stores:
        copy.wait()


def solution(mesh):
    space, dp = mesh.shape["space"], mesh.shape["dp"]
    consts = tables(space)

    def local(fields, lift_weight, mode_weight, local_weight, project_weight, out_cotangent):
        planes = (ROWS, GRID, GRID)
        hbm = pl.BlockSpec(memory_space=pltpu.HBM)
        vmem = pl.BlockSpec(memory_space=pltpu.VMEM)
        share = MODES * MODES // space
        small = [jnp.asarray(c) for c in consts[1:]]
        guess, part, last, team = pl.pallas_call(
            functools.partial(kernel, space, dp),
            out_shape=(
                pltpu.VMEM(planes, BF),
                pltpu.VMEM(planes, BF),
                pltpu.VMEM((space, 128), F32),
                pltpu.VMEM((dp, 128, 128), BF),
            ),
            in_specs=[hbm] * 15,
            out_specs=(vmem, vmem, vmem, vmem),
            scratch_shapes=[
                pltpu.VMEM((256, PIX), BF),
                pltpu.VMEM((MODES, share * CH, CH), BF),
                pltpu.VMEM(planes, BF),
                pltpu.VMEM(planes, BF),
                pltpu.VMEM((ROWS * GRID, GRID), F32),
                pltpu.VMEM((ROWS, PIX), BF),
                pltpu.VMEM((ROWS, PIX), BF),
                pltpu.VMEM((ROWS * GRID, GRID), F32),
                pltpu.VMEM((512, 128), BF),
                pltpu.VMEM((256, TILE), F32),
                pltpu.VMEM((256, TILE), BF),
                pltpu.VMEM((256, TILE), F32),
                pltpu.VMEM((256, TILE), BF),
                pltpu.VMEM((PIX // TILE, 256, TILE), BF),
                pltpu.VMEM((PIX // TILE, 256, TILE), BF),
                pltpu.VMEM((256, 256), F32),
                pltpu.VMEM((256, 256), BF),
                pltpu.VMEM((space * 8, 128), F32),
                pltpu.VMEM((128, 256), F32),
                pltpu.VMEM((space, 1, 128), F32),
                pltpu.VMEM((space, 1, 128), F32),
                pltpu.VMEM((space, 8, 128), BF),
                pltpu.VMEM((space, 8, 128), BF),
                pltpu.VMEM((space, 8, 128), BF),
                pltpu.VMEM((space, 8, 128), BF),
                pltpu.VMEM((space, 1, 128), F32),
                pltpu.VMEM((space, 1, 128), F32),
                pltpu.VMEM((dp, 128, 128), BF),
                pltpu.VMEM((128, 128), F32),
                pltpu.VMEM((FIELDS, CH), BF),
                pltpu.VMEM((CH, CH), BF),
                pltpu.VMEM((FIELDS, CH), BF),
                pltpu.VMEM((128, 64), BF),
                pltpu.VMEM((128, 64), BF),
                pltpu.VMEM((64, 128), BF),
                pltpu.VMEM((64, 128), BF),
                pltpu.VMEM((256, 512), BF),
                pltpu.VMEM((512, 256), BF),
                pltpu.VMEM((256, 128), BF),
                pltpu.VMEM((32, 256), BF),
                pltpu.SemaphoreType.DMA((22,)),
                pltpu.SemaphoreType.DMA((3 + dp,)),
                pltpu.SemaphoreType.DMA((3 + dp,)),
            ],
            compiler_params=pltpu.CompilerParams(
                collective_id=0, has_side_effects=True, vmem_limit_bytes=60 * 1024 * 1024
            ),
        )(
            fields.reshape(planes),
            out_cotangent.reshape(planes),
            mode_weight.reshape(MODES, share * CH, CH),
            jnp.asarray(consts[0]),
            lift_weight,
            local_weight,
            project_weight.T,
            *small[:8],
        )
        prediction, mode_grad, field_grad = pl.pallas_call(
            functools.partial(finish, space, dp),
            out_shape=(
                jax.ShapeDtypeStruct(planes, BF),
                jax.ShapeDtypeStruct((MODES, share * CH, CH), F32),
                jax.ShapeDtypeStruct(planes, BF),
            ),
            in_specs=[vmem] * 6,
            out_specs=(hbm, hbm, hbm),
            scratch_shapes=[
                pltpu.VMEM(planes, BF),
                pltpu.VMEM((MODES, share * CH, CH), F32),
                pltpu.VMEM((512, 128), BF),
                pltpu.SemaphoreType.DMA((6,)),
            ],
            compiler_params=pltpu.CompilerParams(vmem_limit_bytes=32 * 1024 * 1024),
        )(guess, part, last, team, small[6], small[8])
        return (
            prediction.reshape(fields.shape),
            mode_grad.reshape(mode_weight.shape),
            field_grad.reshape(fields.shape),
        )

    wide = P("dp", None, "space", None, None)
    return jax.shard_map(
        local,
        mesh=mesh,
        in_specs=(wide, P(), P(None, "space", None, None), P(), P(), wide),
        out_specs=(wide, P(None, "space", None, None), wide),
        check_vma=False,
    )
```

```python
import functools
import math

import jax
import jax.numpy as jnp
import ml_dtypes
import numpy as np
from jax import lax
from jax.experimental import pallas as pl
from jax.experimental.pallas import tpu as pltpu
from jax.sharding import PartitionSpec as P

F32 = jnp.float32
BF = jnp.bfloat16
MESH = pl.DeviceIdType.MESH

GRID = 128
FIELDS = 8
CH = 64
MODES = 16
PIX = GRID * GRID
ROWS = 32
TILE = 1024
ANA = 1.0 / 512.0
SYN = 8.0 ** -1.5
ROOT = math.sqrt(0.5)


def dot(a, b, dims=((1,), (0,))):
    return lax.dot_general(a, b, (dims, ((), ())), preferred_element_type=F32)


def waves():
    order = np.arange(MODES)
    angle = 2.0 * np.pi * ((order[:, None] + 1) // 2 * np.arange(GRID)[None, :] % GRID) / GRID
    return np.where((order % 2 == 0)[:, None], np.cos(angle), np.sin(angle))


def half(x):
    return np.asarray(x, np.float32).astype(ml_dtypes.bfloat16)


def tables(space):
    w = waves()
    share = MODES * MODES // space
    row = np.arange(MODES * MODES)
    mode = share * (row % space) + row // space
    grid = (w[mode // MODES][:, :, None] * w[mode % MODES][:, None, :]).reshape(MODES * MODES, PIX)
    a0, a1 = w[:, 0::2], w[:, 1::2]
    rep0 = np.repeat(a0, 8, axis=0)
    rep1 = np.repeat(a1, 8, axis=0)
    eye = np.eye(8)
    wave_z = w[mode % MODES]
    pair_y = np.kron(np.eye(2), w)
    kron = np.concatenate([np.kron(a0, eye), np.kron(a1, eye)], axis=0)
    return half(grid), half(rep0), half(rep1), half(rep0.T), half(rep1.T), half(kron), half(kron.T), half(wave_z), half(pair_y), half(pair_y.T)


def iota(shape, axis):
    return lax.broadcasted_iota(jnp.int32, shape, axis)


def activation(w, back):
    twice = 1.0 + lax.erf(w)
    e = jnp.exp2((w * w) * (-1.0 / math.log(2.0)))
    slope = twice + w * (e * (2.0 / math.sqrt(math.pi)))
    return (w * twice).astype(BF), slope.astype(BF) * back


def hops(step):
    x, z, y = step
    return min(x, 4 - x) + min(z, 8 - z) + y


STEPS = sorted(
    [(x, z, y) for x in range(4) for z in range(8) for y in range(2) if x or z or y],
    key=hops, reverse=True,
)


def peers(me):
    x, z, y = me // 16, me // 2 % 8, me % 2
    return [lax.rem(x + dx, 4) * 16 + lax.rem(z + dz, 8) * 2 + lax.rem(y + dy, 2) for dx, dz, dy in STEPS]


def exchange(src, dst, send_sem, recv_sem, me, space):
    for to in peers(me):
        pltpu.make_async_remote_copy(
            src_ref=src.at[to],
            dst_ref=dst.at[me],
            send_sem=send_sem,
            recv_sem=recv_sem,
            device_id={"space": to},
            device_id_type=MESH,
        ).start()
    dst[me] = src[me]


def arrive(src, dst, send_sem, recv_sem, me, space):
    whole = pltpu.make_async_remote_copy(
        src_ref=src.at[pl.ds(0, space - 1)],
        dst_ref=dst.at[pl.ds(0, space - 1)],
        send_sem=send_sem,
        recv_sem=recv_sem,
        device_id={"space": lax.rem(me + 1, space)},
        device_id_type=MESH,
    )
    whole.wait_send()
    whole.wait_recv()


def kernel(
    space, dp,
    f_hbm, c_hbm, w_hbm, t_hbm, lift_hbm, local_hbm, project_hbm,
    rep0_hbm, rep1_hbm, rep0t_hbm, rep1t_hbm, kron_hbm, kront_hbm, wavez_hbm, pairy_hbm,
    pred_ref, part_ref, last_ref, mode_ref,
    t_ref, w_ref, raw_f, raw_c, wide, flat_f, flat_c, part, part_y,
    pre_a, grad_a, pre_b, grad_b, hid, bg, acc, planes, rows_s, stack,
    send1, recv1, send2, recv2, send3, recv3, send4, recv4, team, team_w,
    lift_ref, local_ref, project_ref, rep0_ref, rep1_ref, rep0t_ref, rep1t_ref, kron_ref, kront_ref, wavez_ref, pairy_ref,
    load_sem, send_sem, recv_sem,
):
    me = lax.axis_index("space")
    my_dp = lax.axis_index("dp")
    share = MODES * MODES // space
    chunks = 8
    width = PIX // chunks

    load_f = pltpu.make_async_copy(f_hbm, raw_f, load_sem.at[0])
    load_f.start()
    load_z = pltpu.make_async_copy(wavez_hbm, wavez_ref, load_sem.at[3 + chunks])
    load_z.start()
    load_y = pltpu.make_async_copy(pairy_hbm, pairy_ref, load_sem.at[4 + chunks])
    load_y.start()
    load_s = []
    for n, (src, dst) in enumerate([
        (lift_hbm, lift_ref), (local_hbm, local_ref), (project_hbm, project_ref),
        (rep0_hbm, rep0_ref), (rep1_hbm, rep1_ref), (rep0t_hbm, rep0t_ref), (rep1t_hbm, rep1t_ref),
        (kron_hbm, kron_ref), (kront_hbm, kront_ref),
    ]):
        load_s.append(pltpu.make_async_copy(src, dst, load_sem.at[5 + chunks + n]))
        load_s[-1].start()
    load_t = []
    for n in range(chunks):
        cut = pl.ds(n * width, width)
        load_t.append(pltpu.make_async_copy(t_hbm.at[:, cut], t_ref.at[:, cut], load_sem.at[3 + n]))
        load_t[-1].start()
    load_c = pltpu.make_async_copy(c_hbm, raw_c, load_sem.at[1])
    load_c.start()
    load_w = pltpu.make_async_copy(w_hbm, w_ref, load_sem.at[2])
    load_w.start()

    barrier = pltpu.get_barrier_semaphore()

    for to in peers(me):
        pl.semaphore_signal(barrier, inc=1, device_id={"space": to}, device_id_type=MESH)
    for step in range(1, dp):
        pl.semaphore_signal(barrier, inc=1, device_id={"dp": lax.rem(my_dp + step, dp)}, device_id_type=MESH)

    def relayout(raw, flat):
        def widen(n, carry):
            cut = pl.ds(n * 4, 4)
            wide[pl.ds(pl.multiple_of(n * 512, 512), 512), :] = raw[cut].astype(F32).reshape(512, 128)
            return carry

        lax.fori_loop(0, 8, widen, 0)

        def turn(n, carry):
            for u in range(8):
                y = n * 8 + u
                rows = wide[pl.ds(y, ROWS, stride=GRID), :]
                flat[:, pl.ds(pl.multiple_of(y * GRID, GRID), GRID)] = rows.astype(BF)
            return carry

        lax.fori_loop(0, GRID // 8, turn, 0)

    load_f.wait()
    load_z.wait()
    load_y.wait()
    for n in range(ROWS // 2):
        pair = raw_f[2 * n:2 * n + 2].reshape(2 * GRID, GRID)
        part_y[n * 32:n * 32 + 32, :] = dot(pairy_ref[...], pair).astype(BF)
    value = dot(part_y[...], wavez_ref[...], ((1,), (1,)))
    s_row, s_lane = iota((512, 256), 0), iota((512, 256), 1)
    value = jnp.where(s_row % MODES == s_lane % space // share, value, 0.0).astype(BF)
    fold = (iota((ROWS, 512), 0) == iota((ROWS, 512), 1) // MODES).astype(F32).astype(BF)
    spec = dot(fold, value).T
    send1[...] = jnp.concatenate([spec[b * space:(b + 1) * space] for b in range(share)], axis=1).reshape(space, 1, 128)

    pl.semaphore_wait(barrier, space - 1 + dp - 1)
    exchange(send1, recv1, send_sem.at[0], recv_sem.at[0], me, space)
    for copy in load_s:
        copy.wait()
    lift = lift_ref[...]
    pick32 = (iota((ROWS, FIELDS), 0) // 2 % FIELDS == iota((ROWS, FIELDS), 1)).astype(F32).astype(BF)
    pick128 = (iota((128, FIELDS), 0) // 2 % FIELDS == iota((128, FIELDS), 1)).astype(F32).astype(BF)
    p_row, q_lane = iota((ROWS, 256), 0), iota((ROWS, 256), 1)
    same = (p_row // 16 == q_lane // 128) & (p_row % 2 == q_lane // CH % 2)
    both = dot(lift, local_ref[...])
    both = jnp.concatenate([both[n // 2 % FIELDS:n // 2 % FIELDS + 1] for n in range(ROWS)], axis=0)
    both32 = jnp.where(same, jnp.concatenate([both] * 4, axis=1), 0.0)
    proj32 = dot(pick32, project_ref[...])
    proj32 = jnp.where(same, jnp.concatenate([proj32] * 4, axis=1), 0.0)
    down_field = both32.astype(BF)
    down_proj = proj32.astype(BF)
    up_field = (both32 * ROOT).T.astype(BF)
    up_proj = (proj32 * 0.5).T.astype(BF)
    lift128 = dot(pick128, lift)
    lift_big = jnp.concatenate([lift128] * 4, axis=1)
    lift_bigt = lift_big.T.astype(BF)
    lift_big = lift_big.astype(BF)
    r128, l128 = iota((128, 128), 0), iota((128, 128), 1)
    mask_field = (r128 % 4 == l128 // 32) & (r128 // 4 % 2 == l128 // 16 % 2)
    first_plane = l128 % 2 == 0
    r256, l256 = iota((128, 256), 0), iota((128, 256), 1)
    mask_mode = r256 % 4 == l256 // CH

    relayout(raw_f, flat_f)
    load_c.wait()
    relayout(raw_c, flat_c)
    load_w.wait()
    arrive(send1, recv1, send_sem.at[0], recv_sem.at[0], me, space)

    got = recv1[...].reshape(space, 128).astype(BF)
    coef = jnp.where(first_plane, dot(rep0_ref[...], got), dot(rep1_ref[...], got)) * ANA
    coef = jnp.where(mask_field, coef, 0.0).astype(BF)
    coef = dot(coef, lift_big)
    team_w[:, 0:CH] = coef[:, 0:CH]
    stack[...] = jnp.where(mask_mode, coef, 0.0)
    mixed = []
    for k in range(MODES):
        mixed.append(dot(stack[k * 8:k * 8 + 8, :].astype(BF), w_ref[k]))
    mixed = (jnp.concatenate(mixed, axis=0) * (SYN * ROOT)).astype(BF)
    out = jnp.concatenate(
        [dot(kront_ref[:, 0:128], mixed), dot(kront_ref[:, 128:256], mixed)], axis=1
    )
    send2[...] = out.reshape(space, 8, 128).astype(BF)
    exchange(send2, recv2, send_sem.at[1], recv_sem.at[1], me, space)
    acc[...] = jnp.zeros_like(acc)
    tiles = PIX // TILE

    def up(n, carry):
        cut = pl.ds(pl.multiple_of(n * TILE, TILE), TILE)
        bg[n] = dot(up_proj, flat_c[:, cut]).astype(BF)
        return carry

    lax.fori_loop(0, tiles, up, 0)
    for copy in load_t:
        copy.wait()
    arrive(send2, recv2, send_sem.at[1], recv_sem.at[1], me, space)

    rows_s[...] = recv2[...].astype(F32).reshape(space * 8, 128)
    for s in range(2):
        for b in range(share):
            block = rows_s[pl.ds(s * 4 + b, space, stride=8), :]
            planes[s * 128:(s + 1) * 128, b * space:(b + 1) * space] = block.T.astype(BF)

    def columns(n):
        return pl.ds(pl.multiple_of(n * TILE, TILE), TILE)

    def front(n, pre_s):
        pre_s[...] = dot(planes[...], t_ref[:, columns(n)]) + dot(up_field, flat_f[:, columns(n)])

    def middle(n, pre_s, grad_s):
        for r in range(0, 256, 32):
            for c in range(0, TILE, 512):
                at = (slice(r, r + 32), slice(c, c + 512))
                hidden, grad = activation(pre_s[at], bg[(n,) + at])
                hid[(n,) + at] = hidden
                bg[(n,) + at] = grad
                grad_s[at] = grad

    def back(n, grad_s):
        acc[...] += dot(t_ref[:, columns(n)], grad_s[...], ((1,), (1,)))

    front(0, pre_a)

    def two(n, carry):
        front(2 * n + 1, pre_b)
        middle(2 * n, pre_a, grad_a)
        back(2 * n, grad_a)
        front(jnp.minimum(2 * n + 2, tiles - 1), pre_a)
        middle(2 * n + 1, pre_b, grad_b)
        back(2 * n + 1, grad_b)
        return carry

    lax.fori_loop(0, tiles // 2, two, 0)

    for s in range(2):
        for b in range(share):
            rows_s[pl.ds(s * 4 + b, space, stride=8), :] = acc[b * space:(b + 1) * space, s * 128:(s + 1) * 128]
    send3[...] = rows_s[...].reshape(space, 8, 128).astype(BF)
    exchange(send3, recv3, send_sem.at[2], recv_sem.at[2], me, space)

    def narrow(src, dst):
        def body(n, carry):
            dst[pl.ds(n * 4, 4)] = src[pl.ds(pl.multiple_of(n * 512, 512), 512), :].reshape(4, 128, 128).astype(BF)
            return carry

        lax.fori_loop(0, 8, body, 0)

    def down(n, maps, values, target, scale):
        value = dot(maps, values[n]) * scale
        for u in range(TILE // GRID):
            y = n * (TILE // GRID) + u
            target[pl.ds(y, ROWS, stride=GRID), :] = value[:, u * GRID:(u + 1) * GRID]

    def down_p(n, carry):
        down(n, down_proj, hid, wide, ROOT)
        return carry

    lax.fori_loop(0, tiles, down_p, 0)
    narrow(wide, pred_ref)
    arrive(send3, recv3, send_sem.at[2], recv_sem.at[2], me, space)

    got = recv3[...].astype(F32).reshape(space * 8, 128).astype(BF)
    full = dot(kron_ref[...], got)
    cgrad = (full[0:128, 0:CH] + full[128:256, CH:128]) * SYN
    team_w[:, CH:128] = cgrad
    team[my_dp] = team_w[...].astype(BF)
    copies = []
    for step in range(1, dp):
        copies.append(pltpu.make_async_remote_copy(
            src_ref=team.at[my_dp],
            dst_ref=team.at[my_dp],
            send_sem=send_sem.at[3 + step],
            recv_sem=recv_sem.at[3 + step],
            device_id={"dp": lax.rem(my_dp + step, dp)},
            device_id_type=MESH,
        ))
        copies[-1].start()
    back = []
    for k in range(MODES):
        back.append(dot(cgrad[k * 8:k * 8 + 8, :].astype(BF), w_ref[k], ((1,), (1,))))
    back = jnp.where(mask_mode, jnp.concatenate(back, axis=0), 0.0).astype(BF)
    back = jnp.where(mask_field, dot(back, lift_bigt) * ANA, 0.0).astype(BF)
    lanes = iota((space, 128), 1)
    out = jnp.where(lanes % 2 == 0, dot(rep0t_ref[...], back), dot(rep1t_ref[...], back))
    send4[...] = out.reshape(space, 1, 128)
    exchange(send4, recv4, send_sem.at[3], recv_sem.at[3], me, space)

    def down_f(n, carry):
        down(n, down_field, bg, part, 1.0)
        return carry

    lax.fori_loop(0, tiles, down_f, 0)
    narrow(part, part_ref)
    for copy in copies:
        copy.wait()
    m_row, m_lane = iota((32, 256), 0), iota((32, 256), 1)
    mask_team = m_row % 4 == m_lane // CH
    for k in range(MODES):
        rows = jnp.concatenate([team[d].astype(F32)[k * 8:k * 8 + 8, :] for d in range(dp)], axis=0)
        left = jnp.where(mask_team, jnp.concatenate([rows[:, 0:CH]] * 4, axis=1), 0.0)
        mode_ref[k] = dot(left.T.astype(BF), rows[:, CH:128].astype(BF))
    arrive(send4, recv4, send_sem.at[3], recv_sem.at[3], me, space)
    last_ref[...] = recv4[...].reshape(space, 128)


def finish(
    space, pred, part, last_ref, mode_in, wavez_ref, pairyt_ref,
    pred_hbm, mode_hbm, field_hbm,
    out, inner, store_sem,
):
    share = MODES * MODES // space
    groups = 4
    each = ROWS // groups
    store_p = pltpu.make_async_copy(pred, pred_hbm, store_sem.at[0])
    store_p.start()

    store_m = pltpu.make_async_copy(mode_in, mode_hbm, store_sem.at[1])
    store_m.start()

    turned = last_ref[...].T
    field = jnp.concatenate([turned[b * 32:(b + 1) * 32] for b in range(share)], axis=1).astype(BF)
    spread = (iota((512, ROWS), 0) // MODES == iota((512, ROWS), 1)).astype(F32).astype(BF)
    s_row, s_lane = iota((512, 256), 0), iota((512, 256), 1)
    value = jnp.where(s_row % MODES == s_lane % space // share, dot(spread, field), 0.0).astype(BF)
    inner[...] = dot(value, wavez_ref[...]).astype(BF)
    stores = []
    for g in range(groups):
        for n in range(g * each // 2, (g + 1) * each // 2):
            value = dot(pairyt_ref[...], inner[n * 32:n * 32 + 32, :]).reshape(2, GRID, GRID)
            out[2 * n:2 * n + 2] = (part[2 * n:2 * n + 2].astype(F32) + value).astype(BF)
        cut = pl.ds(g * each, each)
        stores.append(pltpu.make_async_copy(out.at[cut], field_hbm.at[cut], store_sem.at[2 + g]))
        stores[-1].start()
    store_p.wait()
    store_m.wait()
    for copy in stores:
        copy.wait()


def solution(mesh):
    space, dp = mesh.shape["space"], mesh.shape["dp"]
    consts = tables(space)

    def local(fields, lift_weight, mode_weight, local_weight, project_weight, out_cotangent):
        planes = (ROWS, GRID, GRID)
        hbm = pl.BlockSpec(memory_space=pltpu.HBM)
        vmem = pl.BlockSpec(memory_space=pltpu.VMEM)
        share = MODES * MODES // space
        small = [jnp.asarray(c) for c in consts[1:]]
        guess, part, last, mode = pl.pallas_call(
            functools.partial(kernel, space, dp),
            out_shape=(
                pltpu.VMEM(planes, BF),
                pltpu.VMEM(planes, BF),
                pltpu.VMEM((space, 128), F32),
                pltpu.VMEM((MODES, share * CH, CH), F32),
            ),
            in_specs=[hbm] * 15,
            out_specs=(vmem, vmem, vmem, vmem),
            scratch_shapes=[
                pltpu.VMEM((256, PIX), BF),
                pltpu.VMEM((MODES, share * CH, CH), BF),
                pltpu.VMEM(planes, BF),
                pltpu.VMEM(planes, BF),
                pltpu.VMEM((ROWS * GRID, GRID), F32),
                pltpu.VMEM((ROWS, PIX), BF),
                pltpu.VMEM((ROWS, PIX), BF),
                pltpu.VMEM((ROWS * GRID, GRID), F32),
                pltpu.VMEM((512, 128), BF),
                pltpu.VMEM((256, TILE), F32),
                pltpu.VMEM((256, TILE), BF),
                pltpu.VMEM((256, TILE), F32),
                pltpu.VMEM((256, TILE), BF),
                pltpu.VMEM((PIX // TILE, 256, TILE), BF),
                pltpu.VMEM((PIX // TILE, 256, TILE), BF),
                pltpu.VMEM((256, 256), F32),
                pltpu.VMEM((256, 256), BF),
                pltpu.VMEM((space * 8, 128), F32),
                pltpu.VMEM((128, 256), F32),
                pltpu.VMEM((space, 1, 128), F32),
                pltpu.VMEM((space, 1, 128), F32),
                pltpu.VMEM((space, 8, 128), BF),
                pltpu.VMEM((space, 8, 128), BF),
                pltpu.VMEM((space, 8, 128), BF),
                pltpu.VMEM((space, 8, 128), BF),
                pltpu.VMEM((space, 1, 128), F32),
                pltpu.VMEM((space, 1, 128), F32),
                pltpu.VMEM((dp, 128, 128), BF),
                pltpu.VMEM((128, 128), F32),
                pltpu.VMEM((FIELDS, CH), BF),
                pltpu.VMEM((CH, CH), BF),
                pltpu.VMEM((FIELDS, CH), BF),
                pltpu.VMEM((128, 64), BF),
                pltpu.VMEM((128, 64), BF),
                pltpu.VMEM((64, 128), BF),
                pltpu.VMEM((64, 128), BF),
                pltpu.VMEM((256, 512), BF),
                pltpu.VMEM((512, 256), BF),
                pltpu.VMEM((256, 128), BF),
                pltpu.VMEM((32, 256), BF),
                pltpu.SemaphoreType.DMA((22,)),
                pltpu.SemaphoreType.DMA((3 + dp,)),
                pltpu.SemaphoreType.DMA((3 + dp,)),
            ],
            compiler_params=pltpu.CompilerParams(
                collective_id=0, has_side_effects=True, vmem_limit_bytes=59 * 1024 * 1024
            ),
        )(
            fields.reshape(planes),
            out_cotangent.reshape(planes),
            mode_weight.reshape(MODES, share * CH, CH),
            jnp.asarray(consts[0]),
            lift_weight,
            local_weight,
            project_weight.T,
            *small[:8],
        )
        prediction, mode_grad, field_grad = pl.pallas_call(
            functools.partial(finish, space),
            out_shape=(
                jax.ShapeDtypeStruct(planes, BF),
                jax.ShapeDtypeStruct((MODES, share * CH, CH), F32),
                jax.ShapeDtypeStruct(planes, BF),
            ),
            in_specs=[vmem] * 6,
            out_specs=(hbm, hbm, hbm),
            scratch_shapes=[
                pltpu.VMEM(planes, BF),
                pltpu.VMEM((512, 128), BF),
                pltpu.SemaphoreType.DMA((6,)),
            ],
            compiler_params=pltpu.CompilerParams(vmem_limit_bytes=32 * 1024 * 1024),
        )(guess, part, last, mode, small[6], small[8])
        return (
            prediction.reshape(fields.shape),
            mode_grad.reshape(mode_weight.shape),
            field_grad.reshape(fields.shape),
        )

    wide = P("dp", None, "space", None, None)
    return jax.shard_map(
        local,
        mesh=mesh,
        in_specs=(wide, P(), P(None, "space", None, None), P(), P(), wide),
        out_specs=(wide, P(None, "space", None, None), wide),
        check_vma=False,
    )
```

```python
import functools
import math

import jax
import jax.numpy as jnp
import ml_dtypes
import numpy as np
from jax import lax
from jax.experimental import pallas as pl
from jax.experimental.pallas import tpu as pltpu
from jax.sharding import PartitionSpec as P

F32 = jnp.float32
BF = jnp.bfloat16
MESH = pl.DeviceIdType.MESH

GRID = 128
FIELDS = 8
CH = 64
MODES = 16
PIX = GRID * GRID
ROWS = 32
TILE = 1024
ANA = 1.0 / 512.0
SYN = 8.0 ** -1.5
ROOT = math.sqrt(0.5)


def dot(a, b, dims=((1,), (0,))):
    return lax.dot_general(a, b, (dims, ((), ())), preferred_element_type=F32)


def waves():
    order = np.arange(MODES)
    angle = 2.0 * np.pi * ((order[:, None] + 1) // 2 * np.arange(GRID)[None, :] % GRID) / GRID
    return np.where((order % 2 == 0)[:, None], np.cos(angle), np.sin(angle))


def half(x):
    return np.asarray(x, np.float32).astype(ml_dtypes.bfloat16)


def tables(space):
    w = waves()
    share = MODES * MODES // space
    row = np.arange(MODES * MODES)
    mode = share * (row % space) + row // space
    grid = (w[mode // MODES][:, :, None] * w[mode % MODES][:, None, :]).reshape(MODES * MODES, PIX)
    a0, a1 = w[:, 0::2], w[:, 1::2]
    rep0 = np.repeat(a0, 8, axis=0)
    rep1 = np.repeat(a1, 8, axis=0)
    eye = np.eye(8)
    wave_z = w[mode % MODES]
    pair_y = np.kron(np.eye(2), w)
    kron = np.concatenate([np.kron(a0, eye), np.kron(a1, eye)], axis=0)
    return half(grid), half(rep0), half(rep1), half(rep0.T), half(rep1.T), half(kron), half(kron.T), half(wave_z), half(pair_y), half(pair_y.T)


def iota(shape, axis):
    return lax.broadcasted_iota(jnp.int32, shape, axis)


def activation(w, back):
    twice = 1.0 + lax.erf(w)
    e = jnp.exp2((w * w) * (-1.0 / math.log(2.0)))
    slope = twice + w * (e * (2.0 / math.sqrt(math.pi)))
    return (w * twice).astype(BF), slope.astype(BF) * back


def hops(step):
    x, z, y = step
    return min(x, 4 - x) + min(z, 8 - z) + y


STEPS = sorted(
    [(x, z, y) for x in range(4) for z in range(8) for y in range(2) if x or z or y],
    key=hops, reverse=True,
)


def peers(me):
    x, z, y = me // 16, me // 2 % 8, me % 2
    return [lax.rem(x + dx, 4) * 16 + lax.rem(z + dz, 8) * 2 + lax.rem(y + dy, 2) for dx, dz, dy in STEPS]


def exchange(src, dst, send_sem, recv_sem, me, space):
    for to in peers(me):
        pltpu.make_async_remote_copy(
            src_ref=src.at[to],
            dst_ref=dst.at[me],
            send_sem=send_sem,
            recv_sem=recv_sem,
            device_id={"space": to},
            device_id_type=MESH,
        ).start()
    dst[me] = src[me]


def arrive(src, dst, send_sem, recv_sem, me, space):
    whole = pltpu.make_async_remote_copy(
        src_ref=src.at[pl.ds(0, space - 1)],
        dst_ref=dst.at[pl.ds(0, space - 1)],
        send_sem=send_sem,
        recv_sem=recv_sem,
        device_id={"space": lax.rem(me + 1, space)},
        device_id_type=MESH,
    )
    whole.wait_send()
    whole.wait_recv()


def kernel(
    space, dp,
    f_hbm, c_hbm, w_hbm, t_hbm, lift_hbm, local_hbm, project_hbm,
    rep0_hbm, rep1_hbm, rep0t_hbm, rep1t_hbm, kron_hbm, kront_hbm, wavez_hbm, pairy_hbm,
    pred_ref, part_ref, last_ref, mode_ref,
    t_ref, w_ref, raw_f, raw_c, wide, flat_f, flat_c, part, part_y,
    pre_a, grad_a, pre_b, grad_b, hid, bg, acc, planes, rows_s, stack,
    send1, recv1, send2, recv2, send3, recv3, send4, recv4, team, team_w,
    lift_ref, local_ref, project_ref, rep0_ref, rep1_ref, rep0t_ref, rep1t_ref, kron_ref, kront_ref, wavez_ref, pairy_ref,
    load_sem, send_sem, recv_sem,
):
    me = lax.axis_index("space")
    my_dp = lax.axis_index("dp")
    share = MODES * MODES // space
    chunks = 8
    width = PIX // chunks

    load_f = pltpu.make_async_copy(f_hbm, raw_f, load_sem.at[0])
    load_f.start()
    load_z = pltpu.make_async_copy(wavez_hbm, wavez_ref, load_sem.at[3 + chunks])
    load_z.start()
    load_y = pltpu.make_async_copy(pairy_hbm, pairy_ref, load_sem.at[4 + chunks])
    load_y.start()
    load_s = []
    for n, (src, dst) in enumerate([
        (lift_hbm, lift_ref), (local_hbm, local_ref), (project_hbm, project_ref),
        (rep0_hbm, rep0_ref), (rep1_hbm, rep1_ref), (rep0t_hbm, rep0t_ref), (rep1t_hbm, rep1t_ref),
        (kron_hbm, kron_ref), (kront_hbm, kront_ref),
    ]):
        load_s.append(pltpu.make_async_copy(src, dst, load_sem.at[5 + chunks + n]))
        load_s[-1].start()
    load_t = []
    for n in range(chunks):
        cut = pl.ds(n * width, width)
        load_t.append(pltpu.make_async_copy(t_hbm.at[:, cut], t_ref.at[:, cut], load_sem.at[3 + n]))
        load_t[-1].start()
    load_c = pltpu.make_async_copy(c_hbm, raw_c, load_sem.at[1])
    load_c.start()
    load_w = pltpu.make_async_copy(w_hbm, w_ref, load_sem.at[2])
    load_w.start()

    barrier = pltpu.get_barrier_semaphore()

    for to in peers(me):
        pl.semaphore_signal(barrier, inc=1, device_id={"space": to}, device_id_type=MESH)
    for step in range(1, dp):
        pl.semaphore_signal(barrier, inc=1, device_id={"dp": lax.rem(my_dp + step, dp)}, device_id_type=MESH)

    def relayout(raw, flat):
        def widen(n, carry):
            cut = pl.ds(n * 4, 4)
            wide[pl.ds(pl.multiple_of(n * 512, 512), 512), :] = raw[cut].astype(F32).reshape(512, 128)
            return carry

        lax.fori_loop(0, 8, widen, 0)

        def turn(n, carry):
            for u in range(8):
                y = n * 8 + u
                rows = wide[pl.ds(y, ROWS, stride=GRID), :]
                flat[:, pl.ds(pl.multiple_of(y * GRID, GRID), GRID)] = rows.astype(BF)
            return carry

        lax.fori_loop(0, GRID // 8, turn, 0)

    load_f.wait()
    load_z.wait()
    load_y.wait()
    for n in range(ROWS // 2):
        pair = raw_f[2 * n:2 * n + 2].reshape(2 * GRID, GRID)
        part_y[n * 32:n * 32 + 32, :] = dot(pairy_ref[...], pair).astype(BF)
    value = dot(part_y[...], wavez_ref[...], ((1,), (1,)))
    s_row, s_lane = iota((512, 256), 0), iota((512, 256), 1)
    value = jnp.where(s_row % MODES == s_lane % space // share, value, 0.0).astype(BF)
    fold = (iota((ROWS, 512), 0) == iota((ROWS, 512), 1) // MODES).astype(F32).astype(BF)
    spec = dot(fold, value).T
    send1[...] = jnp.concatenate([spec[b * space:(b + 1) * space] for b in range(share)], axis=1).reshape(space, 1, 128)

    pl.semaphore_wait(barrier, space - 1 + dp - 1)
    exchange(send1, recv1, send_sem.at[0], recv_sem.at[0], me, space)
    for copy in load_s:
        copy.wait()
    lift = lift_ref[...]
    pick32 = (iota((ROWS, FIELDS), 0) // 2 % FIELDS == iota((ROWS, FIELDS), 1)).astype(F32).astype(BF)
    pick128 = (iota((128, FIELDS), 0) // 2 % FIELDS == iota((128, FIELDS), 1)).astype(F32).astype(BF)
    p_row, q_lane = iota((ROWS, 256), 0), iota((ROWS, 256), 1)
    same = (p_row // 16 == q_lane // 128) & (p_row % 2 == q_lane // CH % 2)
    both = dot(lift, local_ref[...])
    both = jnp.concatenate([both[n // 2 % FIELDS:n // 2 % FIELDS + 1] for n in range(ROWS)], axis=0)
    both32 = jnp.where(same, jnp.concatenate([both] * 4, axis=1), 0.0)
    proj32 = dot(pick32, project_ref[...])
    proj32 = jnp.where(same, jnp.concatenate([proj32] * 4, axis=1), 0.0)
    down_field = both32.astype(BF)
    down_proj = proj32.astype(BF)
    up_field = (both32 * ROOT).T.astype(BF)
    up_proj = (proj32 * 0.5).T.astype(BF)
    lift128 = dot(pick128, lift)
    lift_big = jnp.concatenate([lift128] * 4, axis=1)
    lift_bigt = lift_big.T.astype(BF)
    lift_big = lift_big.astype(BF)
    r128, l128 = iota((128, 128), 0), iota((128, 128), 1)
    mask_field = (r128 % 4 == l128 // 32) & (r128 // 4 % 2 == l128 // 16 % 2)
    first_plane = l128 % 2 == 0
    r256, l256 = iota((128, 256), 0), iota((128, 256), 1)
    mask_mode = r256 % 4 == l256 // CH

    relayout(raw_f, flat_f)
    load_c.wait()
    relayout(raw_c, flat_c)
    load_w.wait()
    arrive(send1, recv1, send_sem.at[0], recv_sem.at[0], me, space)

    got = recv1[...].reshape(space, 128).astype(BF)
    coef = jnp.where(first_plane, dot(rep0_ref[...], got), dot(rep1_ref[...], got)) * ANA
    coef = jnp.where(mask_field, coef, 0.0).astype(BF)
    coef = dot(coef, lift_big)
    team_w[:, 0:CH] = coef[:, 0:CH]
    stack[...] = jnp.where(mask_mode, coef, 0.0)
    mixed = []
    for k in range(MODES):
        mixed.append(dot(stack[k * 8:k * 8 + 8, :].astype(BF), w_ref[k]))
    mixed = (jnp.concatenate(mixed, axis=0) * (SYN * ROOT)).astype(BF)
    out = jnp.concatenate(
        [dot(kront_ref[:, 0:128], mixed), dot(kront_ref[:, 128:256], mixed)], axis=1
    )
    send2[...] = out.reshape(space, 8, 128).astype(BF)
    exchange(send2, recv2, send_sem.at[1], recv_sem.at[1], me, space)
    acc[...] = jnp.zeros_like(acc)
    tiles = PIX // TILE

    def up(n, carry):
        cut = pl.ds(pl.multiple_of(n * TILE, TILE), TILE)
        bg[n] = dot(up_proj, flat_c[:, cut]).astype(BF)
        return carry

    lax.fori_loop(0, tiles, up, 0)
    for copy in load_t:
        copy.wait()
    arrive(send2, recv2, send_sem.at[1], recv_sem.at[1], me, space)

    rows_s[0:space * 8, :] = recv2[...].astype(F32).reshape(space * 8, 128)
    for s in range(2):
        for b in range(share):
            block = rows_s[pl.ds(s * 4 + b, space, stride=8), :]
            planes[s * 128:(s + 1) * 128, b * space:(b + 1) * space] = block.T.astype(BF)

    def columns(n):
        return pl.ds(pl.multiple_of(n * TILE, TILE), TILE)

    def front(n, pre_s):
        pre_s[...] = dot(planes[...], t_ref[:, columns(n)]) + dot(up_field, flat_f[:, columns(n)])

    def middle(n, pre_s, grad_s):
        for r in range(0, 256, 32):
            for c in range(0, TILE, 512):
                at = (slice(r, r + 32), slice(c, c + 512))
                hidden, grad = activation(pre_s[at], bg[(n,) + at])
                hid[(n,) + at] = hidden
                bg[(n,) + at] = grad
                grad_s[at] = grad

    def back(n, grad_s):
        acc[...] += dot(t_ref[:, columns(n)], grad_s[...], ((1,), (1,)))

    front(0, pre_a)

    def two(n, carry):
        front(2 * n + 1, pre_b)
        middle(2 * n, pre_a, grad_a)
        front(jnp.minimum(2 * n + 2, tiles - 1), pre_a)
        middle(2 * n + 1, pre_b, grad_b)
        back(2 * n, grad_a)
        back(2 * n + 1, grad_b)
        return carry

    lax.fori_loop(0, tiles // 2, two, 0)

    for s in range(2):
        for b in range(share):
            rows_s[pl.ds(s * 4 + b, space, stride=8), :] = acc[b * space:(b + 1) * space, s * 128:(s + 1) * 128]
    send3[...] = rows_s[0:space * 8, :].reshape(space, 8, 128).astype(BF)
    exchange(send3, recv3, send_sem.at[2], recv_sem.at[2], me, space)

    def narrow(src, dst):
        def body(n, carry):
            dst[pl.ds(n * 4, 4)] = src[pl.ds(pl.multiple_of(n * 512, 512), 512), :].reshape(4, 128, 128).astype(BF)
            return carry

        lax.fori_loop(0, 8, body, 0)

    def down(n, maps, values, target, scale):
        value = dot(maps, values[n]) * scale
        for u in range(TILE // GRID):
            y = n * (TILE // GRID) + u
            target[pl.ds(y, ROWS, stride=GRID), :] = value[:, u * GRID:(u + 1) * GRID]

    def down_p(n, carry):
        down(n, down_proj, hid, wide, ROOT)
        return carry

    lax.fori_loop(0, tiles, down_p, 0)
    narrow(wide, pred_ref)
    arrive(send3, recv3, send_sem.at[2], recv_sem.at[2], me, space)

    got = recv3[...].astype(F32).reshape(space * 8, 128).astype(BF)
    full = dot(kron_ref[...], got)
    cgrad = (full[0:128, 0:CH] + full[128:256, CH:128]) * SYN
    team_w[:, CH:128] = cgrad
    team[my_dp] = team_w[...].astype(BF)
    copies = []
    for step in range(1, dp):
        copies.append(pltpu.make_async_remote_copy(
            src_ref=team.at[my_dp],
            dst_ref=team.at[my_dp],
            send_sem=send_sem.at[3 + step],
            recv_sem=recv_sem.at[3 + step],
            device_id={"dp": lax.rem(my_dp + step, dp)},
            device_id_type=MESH,
        ))
        copies[-1].start()
    back = []
    for k in range(MODES):
        back.append(dot(cgrad[k * 8:k * 8 + 8, :].astype(BF), w_ref[k], ((1,), (1,))))
    back = jnp.where(mask_mode, jnp.concatenate(back, axis=0), 0.0).astype(BF)
    back = jnp.where(mask_field, dot(back, lift_bigt) * ANA, 0.0).astype(BF)
    lanes = iota((space, 128), 1)
    out = jnp.where(lanes % 2 == 0, dot(rep0t_ref[...], back), dot(rep1t_ref[...], back))
    send4[...] = out.reshape(space, 1, 128)
    exchange(send4, recv4, send_sem.at[3], recv_sem.at[3], me, space)

    def down_f(n, carry):
        down(n, down_field, bg, part, 1.0)
        return carry

    lax.fori_loop(0, tiles, down_f, 0)
    narrow(part, part_ref)
    for copy in copies:
        copy.wait()
    m_row, m_lane = iota((32, 256), 0), iota((32, 256), 1)
    mask_team = m_row % 4 == m_lane // CH
    for k in range(MODES):
        rows = jnp.concatenate([team[d].astype(F32)[k * 8:k * 8 + 8, :] for d in range(dp)], axis=0)
        left = jnp.where(mask_team, jnp.concatenate([rows[:, 0:CH]] * 4, axis=1), 0.0)
        mode_ref[k] = dot(left.T.astype(BF), rows[:, CH:128].astype(BF))
    arrive(send4, recv4, send_sem.at[3], recv_sem.at[3], me, space)
    last_ref[...] = recv4[...].reshape(space, 128)


def finish(
    space, pred, part, last_ref, mode_in, wavez_ref, pairyt_ref,
    pred_hbm, mode_hbm, field_hbm,
    out, inner, store_sem,
):
    share = MODES * MODES // space
    groups = 4
    each = ROWS // groups
    store_p = pltpu.make_async_copy(pred, pred_hbm, store_sem.at[0])
    store_p.start()

    store_m = pltpu.make_async_copy(mode_in, mode_hbm, store_sem.at[1])
    store_m.start()

    turned = last_ref[...].T
    field = jnp.concatenate([turned[b * 32:(b + 1) * 32] for b in range(share)], axis=1).astype(BF)
    spread = (iota((512, ROWS), 0) // MODES == iota((512, ROWS), 1)).astype(F32).astype(BF)
    s_row, s_lane = iota((512, 256), 0), iota((512, 256), 1)
    value = jnp.where(s_row % MODES == s_lane % space // share, dot(spread, field), 0.0).astype(BF)
    inner[...] = dot(value, wavez_ref[...]).astype(BF)
    stores = []
    for g in range(groups):
        for n in range(g * each // 2, (g + 1) * each // 2):
            value = dot(pairyt_ref[...], inner[n * 32:n * 32 + 32, :]).reshape(2, GRID, GRID)
            out[2 * n:2 * n + 2] = (part[2 * n:2 * n + 2].astype(F32) + value).astype(BF)
        cut = pl.ds(g * each, each)
        stores.append(pltpu.make_async_copy(out.at[cut], field_hbm.at[cut], store_sem.at[2 + g]))
        stores[-1].start()
    store_p.wait()
    store_m.wait()
    for copy in stores:
        copy.wait()


def solution(mesh):
    space, dp = mesh.shape["space"], mesh.shape["dp"]
    consts = tables(space)

    def local(fields, lift_weight, mode_weight, local_weight, project_weight, out_cotangent):
        planes = (ROWS, GRID, GRID)
        hbm = pl.BlockSpec(memory_space=pltpu.HBM)
        vmem = pl.BlockSpec(memory_space=pltpu.VMEM)
        share = MODES * MODES // space
        small = [jnp.asarray(c) for c in consts[1:]]
        guess, part, last, mode = pl.pallas_call(
            functools.partial(kernel, space, dp),
            out_shape=(
                pltpu.VMEM(planes, BF),
                pltpu.VMEM(planes, BF),
                pltpu.VMEM((space, 128), F32),
                pltpu.VMEM((MODES, share * CH, CH), F32),
            ),
            in_specs=[hbm] * 15,
            out_specs=(vmem, vmem, vmem, vmem),
            scratch_shapes=[
                pltpu.VMEM((256, PIX), BF),
                pltpu.VMEM((MODES, share * CH, CH), BF),
                pltpu.VMEM(planes, BF),
                pltpu.VMEM(planes, BF),
                pltpu.VMEM((ROWS * GRID + GRID, GRID), F32),
                pltpu.VMEM((ROWS, PIX), BF),
                pltpu.VMEM((ROWS, PIX), BF),
                pltpu.VMEM((ROWS * GRID + GRID, GRID), F32),
                pltpu.VMEM((512, 128), BF),
                pltpu.VMEM((256, TILE), F32),
                pltpu.VMEM((256, TILE), BF),
                pltpu.VMEM((256, TILE), F32),
                pltpu.VMEM((256, TILE), BF),
                pltpu.VMEM((PIX // TILE, 256, TILE), BF),
                pltpu.VMEM((PIX // TILE, 256, TILE), BF),
                pltpu.VMEM((256, 256), F32),
                pltpu.VMEM((256, 256), BF),
                pltpu.VMEM((space * 8 + 8, 128), F32),
                pltpu.VMEM((128, 256), F32),
                pltpu.VMEM((space, 1, 128), F32),
                pltpu.VMEM((space, 1, 128), F32),
                pltpu.VMEM((space, 8, 128), BF),
                pltpu.VMEM((space, 8, 128), BF),
                pltpu.VMEM((space, 8, 128), BF),
                pltpu.VMEM((space, 8, 128), BF),
                pltpu.VMEM((space, 1, 128), F32),
                pltpu.VMEM((space, 1, 128), F32),
                pltpu.VMEM((dp, 128, 128), BF),
                pltpu.VMEM((128, 128), F32),
                pltpu.VMEM((FIELDS, CH), BF),
                pltpu.VMEM((CH, CH), BF),
                pltpu.VMEM((FIELDS, CH), BF),
                pltpu.VMEM((128, 64), BF),
                pltpu.VMEM((128, 64), BF),
                pltpu.VMEM((64, 128), BF),
                pltpu.VMEM((64, 128), BF),
                pltpu.VMEM((256, 512), BF),
                pltpu.VMEM((512, 256), BF),
                pltpu.VMEM((256, 128), BF),
                pltpu.VMEM((32, 256), BF),
                pltpu.SemaphoreType.DMA((22,)),
                pltpu.SemaphoreType.DMA((3 + dp,)),
                pltpu.SemaphoreType.DMA((3 + dp,)),
            ],
            compiler_params=pltpu.CompilerParams(
                collective_id=0, has_side_effects=True, vmem_limit_bytes=59 * 1024 * 1024
            ),
        )(
            fields.reshape(planes),
            out_cotangent.reshape(planes),
            mode_weight.reshape(MODES, share * CH, CH),
            jnp.asarray(consts[0]),
            lift_weight,
            local_weight,
            project_weight.T,
            *small[:8],
        )
        prediction, mode_grad, field_grad = pl.pallas_call(
            functools.partial(finish, space),
            out_shape=(
                jax.ShapeDtypeStruct(planes, BF),
                jax.ShapeDtypeStruct((MODES, share * CH, CH), F32),
                jax.ShapeDtypeStruct(planes, BF),
            ),
            in_specs=[vmem] * 6,
            out_specs=(hbm, hbm, hbm),
            scratch_shapes=[
                pltpu.VMEM(planes, BF),
                pltpu.VMEM((512, 128), BF),
                pltpu.SemaphoreType.DMA((6,)),
            ],
            compiler_params=pltpu.CompilerParams(vmem_limit_bytes=32 * 1024 * 1024),
        )(guess, part, last, mode, small[6], small[8])
        return (
            prediction.reshape(fields.shape),
            mode_grad.reshape(mode_weight.shape),
            field_grad.reshape(fields.shape),
        )

    wide = P("dp", None, "space", None, None)
    return jax.shard_map(
        local,
        mesh=mesh,
        in_specs=(wide, P(), P(None, "space", None, None), P(), P(), wide),
        out_specs=(wide, P(None, "space", None, None), wide),
        check_vma=False,
    )
```
